32 devices in a mesh: rows: 8 (over z, y), feat: 4 (over x, core).
Axes of the slice: x: 2, y: 2, z: 4, core: 2. Of those that a mesh axis runs over, the one named last changes fastest.
Arguments:
- feats: bfloat16 [256, 16384], P('feat', 'rows'), may hold values from -6 to 6
- weight: bfloat16 [256, 256], P('feat'), may hold values from -0.375 to 0.375
- bias: float32 [256], P('feat'), may hold values from -3 to 3
- tile_cols: int32 [1024], P('rows'), may hold values from 0 to 127, as said below
- tile_values: bfloat16 [1024, 128, 128], P('rows'), may hold values from -0.1875 to 0.1875
- cotangent: bfloat16 [256, 16384], P('feat', 'rows'), may hold values from -6 to 6
Outputs:
- hidden_out: bfloat16 [256, 16384], P('feat', 'rows')
- grad_input: float32 [256, 16384], P('feat', 'rows')
- grad_weight: float32 [256, 256], P('feat')
- grad_bias: float32 [256], P('feat')
The draws below stay inside these ranges and needn't reach their ends.
Inputs may be any that keep to these rules, and one draw needn't show every extreme that they name: `tile_cols`: column blocks of tiles. In each row block the first 4 tiles have column blocks on the same index of rows as the row block (index = column block // 16). Of the other tiles of one index of rows, at most 16 have column blocks on any one index, and in every draw one index receives exactly 16 such tiles from every index.
All inputs are finite; a program needn't handle non-finite values.
Results may differ from the reference program's by a relative error of at most 0.0058.
Values may be sent and summed in bfloat16 or wider, within the bound.
A program may use at most 128 MiB of HBM per device.

```python
import math
import jax
import jax.numpy as jnp
from jax import lax

HID = 256
HID_IN = 256
BLK = 128
TB = 8
TL = 4
R_BLK = 16
REM_DEV = 64
CAP = 16
NTILES = 1024
NODES = 16384
N_ROWS = 8


def draw_tile_cols(key, part):
    common_key, device_key = jax.random.split(jax.random.fold_in(key, 17), 2)
    num_slots = N_ROWS * CAP
    penalty_key, hot_key = jax.random.split(common_key, 2)
    penalty = jax.random.randint(penalty_key, (N_ROWS,), 0, 3)
    hottest = jax.random.randint(hot_key, (), 0, N_ROWS)
    slot_owner = jnp.arange(num_slots) // CAP

    def one_device(dkey, device):
        rank_key, shuffle_key, within_key, local_key = jax.random.split(dkey, 4)
        ranks = jax.random.permutation(rank_key, num_slots)
        score = ranks + penalty[slot_owner] * num_slots
        score = jnp.where(slot_owner == hottest, -1 - jnp.arange(num_slots) % CAP, score)
        chosen = jnp.argsort(score)[:REM_DEV]
        chosen = jax.random.permutation(shuffle_key, chosen)
        owners = chosen // CAP
        within = jax.random.randint(within_key, (REM_DEV,), 0, R_BLK)
        remote = (owners * R_BLK + within).reshape(R_BLK, TB - TL)
        local = device * R_BLK + jax.random.randint(local_key, (R_BLK, TL), 0, R_BLK)
        return jnp.concatenate([local, remote], axis=1).reshape(-1)
    keys = jax.random.split(device_key, N_ROWS)
    result = jax.vmap(one_device)(keys, jnp.arange(N_ROWS))
    return result.reshape(-1).astype(jnp.int32)


def block_scale(key, shape, cuts, least, high):
    factor_of = 1.0
    for dim, shards_of in cuts:
        draws = jax.random.uniform(jax.random.fold_in(jax.random.fold_in(key, 6), dim), (shards_of,), jnp.float32, least / len(cuts), high / len(cuts))
        factor_of = factor_of * jnp.repeat(jnp.exp(draws), shape[dim] // shards_of).reshape((-1,) + (1,) * (len(shape) - 1 - dim))
    return factor_of


def normal_values(stream_key, dims, scale, bound, cuts=(), held_as=jnp.bfloat16):
    entries = jax.random.normal(stream_key, dims, jnp.float32) * scale
    if len(cuts) > 0:
        entries = block_scale(stream_key, dims, cuts, -0.22, 0.18) * entries
    return jnp.clip(entries, min=-bound, max=bound).astype(held_as)


def setup_inputs(seed: int = 0) -> dict:
    streams_of = jax.random.split(jax.random.key(seed), 7)
    return {
        "feats": normal_values(streams_of[0], (HID_IN, NODES), 1.0, 6.0, ((0, 4), (1, 8))),
        "weight": normal_values(streams_of[1], (HID_IN, HID), HID_IN ** -0.5, 0.375, ((0, 4),)),
        "bias": normal_values(streams_of[2], (HID,), 0.5, 3.0, ((0, 4),), jnp.float32),
        "tile_cols": draw_tile_cols(jax.random.fold_in(streams_of[6], 71), 0),
        "tile_values": normal_values(streams_of[4], (NTILES, BLK, BLK), (TB * BLK) ** -0.5, 0.1875, ((0, 8),)),
        "cotangent": normal_values(streams_of[5], (HID, NODES), 1.0, 6.0, ((0, 4), (1, 8))),
    }


def reference(feats, weight, bias, tile_cols, tile_values, cotangent):
    nodes = feats.shape[1]
    block_count = nodes // BLK
    proj = jnp.dot(weight.T, feats, preferred_element_type=jnp.float32).astype(jnp.bfloat16)
    proj_blocks = proj.reshape(HID, block_count, BLK).transpose(1, 0, 2)
    col_groups = tile_cols.reshape(N_ROWS, R_BLK, TB).astype(jnp.int32)
    value_groups = tile_values.reshape(N_ROWS, R_BLK, TB, BLK, BLK)

    def forward_group(pair):
        columns, values = pair
        fetched = proj_blocks[columns].astype(jnp.float32)
        return jnp.einsum('btfk,btnk->bfn', fetched, values.astype(jnp.float32))
    summed = lax.map(forward_group, (col_groups, value_groups)).reshape(block_count, HID, BLK)
    pre = summed.transpose(1, 0, 2).reshape(HID, nodes) + bias[:, None]
    hidden_out = jax.nn.silu(pre).astype(jnp.bfloat16)
    sigma = jax.nn.sigmoid(pre)
    grad_pre = cotangent.astype(jnp.float32) * (sigma * (1.0 + pre * (1.0 - sigma)))
    grad_blocks = grad_pre.astype(jnp.bfloat16).reshape(HID, block_count, BLK).transpose(1, 0, 2)
    grad_blocks = grad_blocks.reshape(N_ROWS, R_BLK, HID, BLK)

    def backward_group(total, triple):
        columns, values, grads = triple
        contrib = jnp.einsum('bfn,btnk->btfk', grads.astype(jnp.float32), values.astype(jnp.float32))
        return (total.at[columns.reshape(-1)].add(contrib.reshape(-1, HID, BLK)), None)
    start_total = jnp.zeros((block_count, HID, BLK), jnp.float32)
    grad_proj_blocks, _ = lax.scan(backward_group, start_total, (col_groups, value_groups, grad_blocks))
    grad_proj = grad_proj_blocks.transpose(1, 0, 2).reshape(HID, nodes).astype(jnp.bfloat16)
    grad_input = jnp.dot(weight, grad_proj, preferred_element_type=jnp.float32)
    grad_weight = jnp.dot(feats, grad_proj.T, preferred_element_type=jnp.float32) / math.sqrt(nodes)
    grad_bias = lax.optimization_barrier(jnp.sum(grad_pre, axis=1)) / math.sqrt(nodes)
    return (hidden_out, grad_input, grad_weight, grad_bias)
```

```python
import functools
import math

import jax
import jax.numpy as jnp
from jax import lax
from jax.experimental import pallas as pl
from jax.experimental.pallas import tpu as pltpu
from jax.sharding import PartitionSpec as P

MESH = pl.DeviceIdType.MESH
F32 = jnp.float32
BF16 = jnp.bfloat16


def kernel(
    n,
    chunks,
    sum_inside,
    scale,
    cols,
    order,
    order_row,
    keep,
    last,
    has,
    feats,
    weight,
    bias,
    tiles_hbm,
    cot_hbm,
    hidden,
    grad_in,
    grad_w,
    grad_b,
    gbuf,
    tiles,
    cot,
    zall,
    gall,
    ubuf,
    sbuf,
    back,
    wall,
    wt,
    bias_acc,
    wsum,
    wland,
    wpiece,
    local_sem,
    w_send,
    w_recv,
    ag_send,
    ag_recv,
    fe_send,
    fe_recv,
    rs_send,
    rs_recv,
    s1_send,
    s1_recv,
    s2_send,
    s2_recv,
):
    width, nodes = feats.shape
    block = tiles.shape[1]
    row_blocks = nodes // block
    per_block = tiles.shape[0] // row_blocks
    in_chunk = row_blocks // chunks
    cw = in_chunk * block
    half = n // 2
    row = lax.axis_index("rows")
    fe = lax.axis_index("feat")
    odd = lax.rem(row, 2)
    pos = (1 - odd) * (row // 2) + odd * (n - 1 - row // 2)

    def row_at(p):
        p = lax.rem(p + 2 * n, n)
        far = p // half
        return (1 - far) * (2 * p) + far * (2 * n - 1 - 2 * p)

    near = (row_at(pos + 1), row_at(pos - 1))
    sib = fe + 1 - 2 * lax.rem(fe, 2)
    opp = lax.rem(fe + 2, 4)
    opp_sib = lax.rem(sib + 2, 4)

    tile_copy = pltpu.make_async_copy(tiles_hbm, tiles, local_sem.at[0])
    cot_copy = pltpu.make_async_copy(cot_hbm, cot, local_sem.at[1])
    tile_copy.start()
    cot_copy.start()

    barrier = pltpu.get_barrier_semaphore()
    if sum_inside:
        others = [lax.rem(row + k, n) for k in range(1, n)]
    else:
        others = list(near)
    for peer in others:
        pl.semaphore_signal(barrier, inc=1, device_id={"rows": peer}, device_id_type=MESH)
    for peer in (sib, opp, opp_sib):
        pl.semaphore_signal(barrier, inc=1, device_id={"feat": peer}, device_id_type=MESH)

    for b in range(row_blocks):
        gbuf[row * row_blocks + b] = feats[:, b * block : (b + 1) * block]
    wall[pl.ds(pl.multiple_of(fe * width, width), width), :] = weight[...]
    pl.semaphore_wait(barrier, len(others) + 3)

    def span(owner, c):
        return gbuf.at[pl.ds(owner * row_blocks + c * in_chunk, in_chunk)]

    def gather_copy(way, d, c):
        sign = 1 - 2 * way
        at = span(row_at(pos - sign * d), c)
        return pltpu.make_async_remote_copy(
            src_ref=at,
            dst_ref=at,
            send_sem=ag_send.at[way, d, c],
            recv_sem=ag_recv.at[way, d, c],
            device_id={"rows": near[way]},
            device_id_type=MESH,
        )

    def gather_arrival(way, d, c):
        sign = 1 - 2 * way
        at = span(row_at(pos - sign * (d + 1)), c)
        return pltpu.make_async_remote_copy(
            src_ref=at,
            dst_ref=at,
            send_sem=ag_send.at[way, d, c],
            recv_sem=ag_recv.at[way, d, c],
            device_id={"rows": near[way]},
            device_id_type=MESH,
        )

    def moves(way, d):
        if d < half - 1:
            return list(range(chunks))
        if way == 0:
            return list(range(chunks // 2))
        return list(range(chunks // 2, chunks))

    def weight_copy(k, peer):
        at = wall.at[pl.ds(pl.multiple_of(fe * width, width), width), :]
        return pltpu.make_async_remote_copy(
            src_ref=at,
            dst_ref=at,
            send_sem=w_send.at[k],
            recv_sem=w_recv.at[k],
            device_id={"feat": peer},
            device_id_type=MESH,
        )

    def weight_arrival(k, peer):
        at = wall.at[pl.ds(pl.multiple_of(peer * width, width), width), :]
        return pltpu.make_async_remote_copy(
            src_ref=at,
            dst_ref=at,
            send_sem=w_send.at[k],
            recv_sem=w_recv.at[k],
            device_id={"feat": peer},
            device_id_type=MESH,
        )

    for c in range(chunks):
        for way in range(2):
            if c in moves(way, 0):
                gather_copy(way, 0, c).start()
    for k, peer in enumerate((sib, opp, opp_sib)):
        weight_copy(k, peer).start()
    for d in range(1, half):
        for c in range(chunks):
            for way in range(2):
                if c in moves(way, d - 1):
                    gather_arrival(way, d - 1, c).wait_recv()
                if c in moves(way, d):
                    gather_copy(way, d, c).start()
        if d == 1:
            for k, peer in enumerate((sib, opp, opp_sib)):
                weight_arrival(k, peer).wait_recv()
            wt[...] = wall[...].astype(F32).T.astype(BF16)
            tile_copy.wait()
            cot_copy.wait()
    for way in range(2):
        for c in moves(way, half - 1):
            gather_arrival(way, half - 1, c).wait_recv()

    def feat_move(buf, kind, hop, c, owner, peer):
        at = buf.at[c, pl.ds(pl.multiple_of(owner * width, width), width), :]
        return pltpu.make_async_remote_copy(
            src_ref=at,
            dst_ref=at,
            send_sem=fe_send.at[kind, hop, c],
            recv_sem=fe_recv.at[kind, hop, c],
            device_id={"feat": peer},
            device_id_type=MESH,
        )

    def feat_start(buf, kind, c):
        feat_move(buf, kind, 0, c, fe, opp).start()
        feat_move(buf, kind, 1, c, fe, sib).start()

    def feat_pass(buf, kind, c):
        feat_move(buf, kind, 0, c, opp, opp).wait_recv()
        feat_move(buf, kind, 2, c, opp, sib).start()

    def feat_arrive(buf, kind, c):
        feat_move(buf, kind, 1, c, sib, sib).wait_recv()
        feat_move(buf, kind, 2, c, opp_sib, sib).wait_recv()

    mine = pl.ds(pl.multiple_of(fe * width, width), width)

    for c in range(chunks):

        def one_row(r, carry, c=c):
            total = jnp.zeros((width, block), F32)
            for t in range(per_block):
                i = (c * in_chunk + r) * per_block + t
                total += lax.dot_general(
                    gbuf[cols[i]], tiles[i], (((1,), (1,)), ((), ())), preferred_element_type=F32
                )
            zall[c, mine, pl.ds(pl.multiple_of(r * block, block), block)] = total.astype(BF16)
            return carry

        lax.fori_loop(0, in_chunk, one_row, 0)
        feat_start(zall, 0, c)
        if c > 0:
            feat_pass(zall, 0, c - 1)
    feat_pass(zall, 0, chunks - 1)

    w_cols = wt[mine, :]
    for c in range(chunks):
        feat_arrive(zall, 0, c)
        pre = jnp.dot(w_cols, zall[c], preferred_element_type=F32) + bias[...]
        sigma = jax.nn.sigmoid(pre)
        hidden[:, c * cw : (c + 1) * cw] = (pre * sigma).astype(BF16)
        g = cot[:, c * cw : (c + 1) * cw].astype(F32) * (sigma * (1.0 + pre * (1.0 - sigma)))
        gall[c, mine, :] = g.astype(BF16)
        feat_start(gall, 1, c)
        folded = g[:, :block]
        for b in range(1, in_chunk):
            folded = folded + g[:, b * block : (b + 1) * block]
        bias_acc[...] = folded if c == 0 else bias_acc[...] + folded
        if c > 0:
            feat_pass(gall, 1, c - 1)
    feat_pass(gall, 1, chunks - 1)

    w_sum = jnp.zeros((width, wall.shape[1]), F32)
    for c in range(chunks):
        feat_arrive(gall, 1, c)
        u = jnp.dot(weight[...], gall[c], preferred_element_type=F32).astype(BF16)
        for b in range(in_chunk):
            ubuf[c * in_chunk + b] = u[:, b * block : (b + 1) * block]
        w_sum += lax.dot_general(
            zall[c, mine, :], gall[c], (((1,), (1,)), ((), ())), preferred_element_type=F32
        )
    hid = wall.shape[1]
    wsum[:, :hid] = w_sum
    wsum[:, hid:] = jnp.broadcast_to(jnp.sum(bias_acc[...], axis=1, keepdims=True), bias_acc.shape)

    piece = width // n if sum_inside else width

    def piece_at(ref, owner):
        return ref.at[pl.ds(pl.multiple_of(owner * piece, piece), piece), :]

    def piece_copy(k):
        to = lax.rem(row + k, n)
        return pltpu.make_async_remote_copy(
            src_ref=piece_at(wsum, to),
            dst_ref=wland.at[k],
            send_sem=s1_send.at[k],
            recv_sem=s1_recv.at[k],
            device_id={"rows": to},
            device_id_type=MESH,
        )

    def total_copy(k):
        to = lax.rem(row + k, n)
        return pltpu.make_async_remote_copy(
            src_ref=piece_at(wpiece, row),
            dst_ref=piece_at(wpiece, row),
            send_sem=s2_send.at[k],
            recv_sem=s2_recv.at[k],
            device_id={"rows": to},
            device_id_type=MESH,
        )

    def total_arrival(k):
        owner = lax.rem(row + n - k, n)
        return pltpu.make_async_remote_copy(
            src_ref=piece_at(wpiece, owner),
            dst_ref=piece_at(wpiece, owner),
            send_sem=s2_send.at[k],
            recv_sem=s2_recv.at[k],
            device_id={"rows": owner},
            device_id_type=MESH,
        )

    if sum_inside:
        for k in range(1, n):
            piece_copy(k).start()

    group = 8

    def some_terms(i, running):
        for j in range(group):
            at = i * group + j
            sbuf[at] = jnp.dot(
                ubuf[order_row[at]], tiles[order[at]], preferred_element_type=F32
            )
        for j in range(group):
            at = i * group + j
            running = sbuf[at] + keep[at] * running
            sbuf[at] = running
        return running

    lax.fori_loop(0, tiles.shape[0] // group, some_terms, jnp.zeros((width, block), F32))

    for way in range(2):
        for d in range(half):
            for c in moves(way, d):
                gather_copy(way, d, c).wait_send()

    def own_term(at):
        return sbuf[last[at]] * has[at]

    def back_copy(way, d, c):
        sign = 1 - 2 * way
        return pltpu.make_async_remote_copy(
            src_ref=span(row_at(pos + sign * d), c),
            dst_ref=back.at[way, d - 1, pl.ds(c * in_chunk, in_chunk)],
            send_sem=rs_send.at[way, d - 1, c],
            recv_sem=rs_recv.at[way, d - 1, c],
            device_id={"rows": near[way]},
            device_id_type=MESH,
        )

    for d in range(half, 0, -1):
        for c in range(chunks):
            for way in range(2):
                if c not in moves(way, d - 1):
                    continue
                joined = d < half and c in moves(way, d)
                if joined:
                    back_copy(way, d + 1, c).wait_recv()
                sign = 1 - 2 * way
                owner = row_at(pos + sign * d)
                for b in range(c * in_chunk, (c + 1) * in_chunk):
                    at = owner * row_blocks + b
                    value = own_term(at)
                    if joined:
                        value = value + back[way, d, b].astype(F32)
                    gbuf[at] = value.astype(BF16)
                back_copy(way, d, c).start()
        if sum_inside and d == half - 1:
            whole = wsum[pl.ds(pl.multiple_of(row * piece, piece), piece), :]
            for k in range(1, n):
                piece_copy(k).wait_recv()
                whole = whole + wland[k]
            wpiece[pl.ds(pl.multiple_of(row * piece, piece), piece), :] = whole * scale
            for k in range(1, n):
                total_copy(k).start()

    for c in range(chunks):
        for way in range(2):
            back_copy(way, 1, c).wait_recv()
        for b in range(c * in_chunk, (c + 1) * in_chunk):
            value = own_term(row * row_blocks + b)
            value = value + back[0, 0, b].astype(F32) + back[1, 0, b].astype(F32)
            grad_in[:, b * block : (b + 1) * block] = value

    if sum_inside:
        for k in range(1, n):
            total_arrival(k).wait_recv()
        grad_w[...] = wpiece[:, :hid]
        grad_b[...] = wpiece[:, hid:]
    else:
        grad_w[...] = wsum[:, :hid]
        grad_b[...] = wsum[:, hid:]

    for k, peer in enumerate((sib, opp, opp_sib)):
        weight_copy(k, peer).wait_send()
    for kind, buf in enumerate((zall, gall)):
        for c in range(chunks):
            feat_move(buf, kind, 0, c, fe, opp).wait_send()
            feat_move(buf, kind, 1, c, fe, sib).wait_send()
            feat_move(buf, kind, 2, c, opp, sib).wait_send()
    for way in range(2):
        for d in range(1, half + 1):
            for c in moves(way, d - 1):
                back_copy(way, d, c).wait_send()
    if sum_inside:
        for k in range(1, n):
            piece_copy(k).wait_send()
            total_copy(k).wait_send()


def local(feats, weight, bias, tile_cols, tile_values, cotangent):
    width, nodes = feats.shape
    hid = weight.shape[1]
    count, block = tile_values.shape[0], tile_values.shape[1]
    n = lax.axis_size("rows")
    row_blocks = nodes // block
    per_block = count // row_blocks
    chunks = 4 if n <= 8 else 2
    half = n // 2
    sum_inside = n == 8
    scale = 1.0 / math.sqrt(nodes * n)

    index = jnp.arange(count, dtype=jnp.int32)
    earlier = (tile_cols[None, :] < tile_cols[:, None]) | (
        (tile_cols[None, :] == tile_cols[:, None]) & (index[None, :] < index[:, None])
    )
    rank = jnp.sum(earlier.astype(jnp.int32), axis=1)
    placed = rank[None, :] == index[:, None]
    order = jnp.sum(jnp.where(placed, index[None, :], 0), axis=1)
    order_row = order // per_block
    in_order = jnp.sum(jnp.where(placed, tile_cols[None, :], 0), axis=1)
    keep = jnp.concatenate([jnp.zeros((1,), F32), (in_order[1:] == in_order[:-1]).astype(F32)])
    dest = jnp.arange(n * row_blocks, dtype=jnp.int32)
    upto = jnp.sum((tile_cols[None, :] <= dest[:, None]).astype(jnp.int32), axis=1)
    below = jnp.sum((tile_cols[None, :] < dest[:, None]).astype(jnp.int32), axis=1)
    has = (upto > below).astype(F32)
    last = jnp.maximum(upto - 1, 0)

    smem = pl.BlockSpec(memory_space=pltpu.SMEM)
    vmem = pl.BlockSpec(memory_space=pltpu.VMEM)
    anywhere = pl.BlockSpec(memory_space=pl.ANY)
    dma = pltpu.SemaphoreType.DMA
    piece = width // n if sum_inside else 8
    hidden, grad_in, grad_w, grad_b = pl.pallas_call(
        functools.partial(kernel, n, chunks, sum_inside, scale),
        out_shape=(
            jax.ShapeDtypeStruct((width, nodes), BF16),
            jax.ShapeDtypeStruct((width, nodes), F32),
            jax.ShapeDtypeStruct((width, hid), F32),
            jax.ShapeDtypeStruct((width, block), F32),
        ),
        in_specs=[smem] * 6 + [vmem] * 3 + [anywhere] * 2,
        out_specs=(vmem,) * 4,
        scratch_shapes=[
            pltpu.VMEM((n * row_blocks, width, block), BF16),
            pltpu.VMEM((count, block, block), BF16),
            pltpu.VMEM((width, nodes), BF16),
            pltpu.VMEM((chunks, 4 * width, nodes // chunks), BF16),
            pltpu.VMEM((chunks, 4 * width, nodes // chunks), BF16),
            pltpu.VMEM((row_blocks, width, block), BF16),
            pltpu.VMEM((count, width, block), F32),
            pltpu.VMEM((2, half, row_blocks, width, block), BF16),
            pltpu.VMEM((4 * width, hid), BF16),
            pltpu.VMEM((hid, 4 * width), BF16),
            pltpu.VMEM((width, block), F32),
            pltpu.VMEM((width, hid + block), F32),
            pltpu.VMEM((n if sum_inside else 1, piece, hid + block), F32),
            pltpu.VMEM((width, hid + block), F32),
            dma((2,)),
            dma((3,)),
            dma((3,)),
            dma((2, half, chunks)),
            dma((2, half, chunks)),
            dma((2, 3, chunks)),
            dma((2, 3, chunks)),
            dma((2, half, chunks)),
            dma((2, half, chunks)),
            dma((n,)),
            dma((n,)),
            dma((n,)),
            dma((n,)),
        ],
        compiler_params=pltpu.CompilerParams(
            collective_id=0, has_side_effects=True, vmem_limit_bytes=52 * 1024 * 1024
        ),
        cost_estimate=pl.CostEstimate(
            flops=2 * 2 * count * width * block * block + 6 * width * hid * nodes,
            bytes_accessed=2 * count * block * block,
            transcendentals=width * nodes,
        ),
    )(
        tile_cols,
        order,
        order_row,
        keep,
        last,
        has,
        feats,
        weight,
        bias[:, None],
        tile_values,
        cotangent,
    )
    bias_total = grad_b[:, 0]
    if not sum_inside:
        grad_w, bias_total = lax.psum((grad_w * scale, bias_total * scale), "rows")
    return hidden, grad_in, grad_w, bias_total


def solution(mesh):
    placed = (
        P("feat", "rows"),
        P("feat", None),
        P("feat"),
        P("rows"),
        P("rows", None, None),
        P("feat", "rows"),
    )
    return jax.shard_map(
        local,
        mesh=mesh,
        in_specs=placed,
        out_specs=(P("feat", "rows"), P("feat", "rows"), P("feat", None), P("feat")),
        check_vma=False,
    )
```

```python
import functools
import math

import jax
import jax.numpy as jnp
from jax import lax
from jax.experimental import pallas as pl
from jax.experimental.pallas import tpu as pltpu
from jax.sharding import PartitionSpec as P

MESH = pl.DeviceIdType.MESH
TL = 4
F32 = jnp.float32
BF16 = jnp.bfloat16


def kernel(
    n,
    chunks,
    sum_inside,
    scale,
    cols,
    order,
    keep,
    last,
    has,
    bias,
    feats,
    weight,
    tiles_hbm,
    cot_hbm,
    hidden_hbm,
    grad_in_hbm,
    grad_w_hbm,
    grad_b,
    own,
    gbuf,
    tiles,
    cot,
    zall,
    gall,
    ubuf,
    tbuf,
    sbuf,
    zloc,
    hidden,
    grad_in,
    back,
    wall,
    wt,
    bias_acc,
    wsum,
    wland,
    wpiece,
    local_sem,
    feats_sem,
    out_sem,
    w_send,
    w_recv,
    ag_send,
    ag_recv,
    fe_send,
    fe_recv,
    rs_send,
    rs_recv,
    s1_send,
    s1_recv,
    s2_send,
    s2_recv,
):
    width, nodes = feats.shape
    block = tiles.shape[1]
    row_blocks = nodes // block
    per_block = tiles.shape[0] // row_blocks
    in_chunk = row_blocks // chunks
    cw = in_chunk * block
    half = n // 2
    row = lax.axis_index("rows")
    fe = lax.axis_index("feat")
    odd = lax.rem(row, 2)
    pos = (1 - odd) * (row // 2) + odd * (n - 1 - row // 2)

    def row_at(p):
        p = lax.rem(p + 2 * n, n)
        far = p // half
        return (1 - far) * (2 * p) + far * (2 * n - 1 - 2 * p)

    near = (row_at(pos + 1), row_at(pos - 1))
    sib = fe + 1 - 2 * lax.rem(fe, 2)
    opp = lax.rem(fe + 2, 4)
    opp_sib = lax.rem(sib + 2, 4)

    tile_copy = pltpu.make_async_copy(tiles_hbm, tiles, local_sem.at[0])
    cot_copy = pltpu.make_async_copy(cot_hbm, cot, local_sem.at[1])
    feats_copies = [
        pltpu.make_async_copy(
            feats.at[:, pl.ds(b * block, block)],
            own.at[b],
            feats_sem.at[b],
        )
        for b in range(row_blocks)
    ]
    for copy in feats_copies:
        copy.start()
    mine = pl.ds(pl.multiple_of(fe * width, width), width)
    weight_in = pltpu.make_async_copy(weight, wall.at[mine, :], local_sem.at[2])
    weight_in.start()

    barrier = pltpu.get_barrier_semaphore()
    if sum_inside:
        others = [lax.rem(row + k, n) for k in range(1, n)]
    else:
        others = list(near)
    for peer in others:
        pl.semaphore_signal(barrier, inc=1, device_id={"rows": peer}, device_id_type=MESH)
    for peer in (sib, opp, opp_sib):
        pl.semaphore_signal(barrier, inc=1, device_id={"feat": peer}, device_id_type=MESH)

    for copy in feats_copies:
        copy.wait()
    tile_copy.start()
    cot_copy.start()
    weight_in.wait()
    pl.semaphore_wait(barrier, len(others) + 3)

    def span(owner, c):
        return gbuf.at[pl.ds(owner * row_blocks + c * in_chunk, in_chunk)]

    def gather_copy(way, d, c):
        sign = 1 - 2 * way
        at = span(row_at(pos - sign * d), c)
        src = own.at[pl.ds(c * in_chunk, in_chunk)] if d == 0 else at
        return pltpu.make_async_remote_copy(
            src_ref=src,
            dst_ref=at,
            send_sem=ag_send.at[way, d, c],
            recv_sem=ag_recv.at[way, d, c],
            device_id={"rows": near[way]},
            device_id_type=MESH,
        )

    def gather_arrival(way, d, c):
        sign = 1 - 2 * way
        at = span(row_at(pos - sign * (d + 1)), c)
        return pltpu.make_async_remote_copy(
            src_ref=at,
            dst_ref=at,
            send_sem=ag_send.at[way, d, c],
            recv_sem=ag_recv.at[way, d, c],
            device_id={"rows": near[way]},
            device_id_type=MESH,
        )

    def moves(way, d):
        if d < half - 1:
            return list(range(chunks))
        if way == 0:
            return list(range(chunks // 2))
        return list(range(chunks // 2, chunks))

    def weight_copy(k, peer):
        at = wall.at[pl.ds(pl.multiple_of(fe * width, width), width), :]
        return pltpu.make_async_remote_copy(
            src_ref=at,
            dst_ref=at,
            send_sem=w_send.at[k],
            recv_sem=w_recv.at[k],
            device_id={"feat": peer},
            device_id_type=MESH,
        )

    def weight_arrival(k, peer):
        at = wall.at[pl.ds(pl.multiple_of(peer * width, width), width), :]
        return pltpu.make_async_remote_copy(
            src_ref=at,
            dst_ref=at,
            send_sem=w_send.at[k],
            recv_sem=w_recv.at[k],
            device_id={"feat": peer},
            device_id_type=MESH,
        )

    for c in range(chunks):
        for way in range(2):
            if c in moves(way, 0):
                gather_copy(way, 0, c).start()
    for k, peer in enumerate((sib, opp, opp_sib)):
        weight_copy(k, peer).start()
    def products(get, r, first, count):
        left = jnp.concatenate([get(r * per_block + first + t) for t in range(count)], axis=1)
        right = jnp.concatenate([tiles[r * per_block + first + t] for t in range(count)], axis=1)
        return lax.dot_general(left, right, (((1,), (1,)), ((), ())), preferred_element_type=F32)

    def local_products(r):
        zloc[r] = products(lambda i: own[cols[i]], r, 0, TL)

    for b in range(row_blocks):
        gbuf[row * row_blocks + b] = own[b]
    done = 0
    for d in range(1, half):
        for c in range(chunks):
            for way in range(2):
                if c in moves(way, d - 1):
                    gather_arrival(way, d - 1, c).wait_recv()
                if c in moves(way, d):
                    gather_copy(way, d, c).start()
            if d == 1 and c == 0:
                tile_copy.wait()
            if done < row_blocks:
                for r in range(done, min(done + 2, row_blocks)):
                    local_products(r)
                done = min(done + 2, row_blocks)
        if d == 1:
            for k, peer in enumerate((sib, opp, opp_sib)):
                weight_arrival(k, peer).wait_recv()
            wt[...] = wall[...].astype(F32).T.astype(BF16)
            cot_copy.wait()
    for r in range(done, row_blocks):
        local_products(r)
    for way in range(2):
        for c in moves(way, half - 1):
            gather_arrival(way, half - 1, c).wait_recv()

    def feat_move(buf, kind, hop, c, owner, peer):
        at = buf.at[c, pl.ds(pl.multiple_of(owner * width, width), width), :]
        return pltpu.make_async_remote_copy(
            src_ref=at,
            dst_ref=at,
            send_sem=fe_send.at[kind, hop, c],
            recv_sem=fe_recv.at[kind, hop, c],
            device_id={"feat": peer},
            device_id_type=MESH,
        )

    def feat_start(buf, kind, c):
        feat_move(buf, kind, 0, c, fe, opp).start()
        feat_move(buf, kind, 1, c, fe, sib).start()

    def feat_pass(buf, kind, c):
        feat_move(buf, kind, 0, c, opp, opp).wait_recv()
        feat_move(buf, kind, 2, c, opp, sib).start()

    def feat_arrive(buf, kind, c):
        feat_move(buf, kind, 1, c, sib, sib).wait_recv()
        feat_move(buf, kind, 2, c, opp_sib, sib).wait_recv()

    for c in range(chunks):

        def one_row(r, carry, c=c):
            at = c * in_chunk + r
            total = zloc[at] + products(lambda i: gbuf[cols[i]], at, TL, per_block - TL)
            zall[c, mine, pl.ds(pl.multiple_of(r * block, block), block)] = total.astype(BF16)
            return carry

        lax.fori_loop(0, in_chunk, one_row, 0)
        feat_start(zall, 0, c)
        if c > 0:
            feat_pass(zall, 0, c - 1)
    feat_pass(zall, 0, chunks - 1)

    w_cols = wt[mine, :]
    w_rows = wall[mine, :]
    diagonal = lax.broadcasted_iota(jnp.int32, (width, width), 0) == lax.broadcasted_iota(
        jnp.int32, (width, width), 1
    )
    bias_row = jnp.broadcast_to(bias[...], (width, width))
    bias_col = jnp.sum(jnp.where(diagonal, bias_row, 0.0), axis=1, keepdims=True)
    for c in range(chunks):
        feat_arrive(zall, 0, c)
        pre = jnp.dot(w_cols, zall[c], preferred_element_type=F32) + bias_col
        sigma = jax.nn.sigmoid(pre)
        hidden[:, c * cw : (c + 1) * cw] = (pre * sigma).astype(BF16)
        g = cot[:, c * cw : (c + 1) * cw].astype(F32) * (sigma * (1.0 + pre * (1.0 - sigma)))
        gall[c, mine, :] = g.astype(BF16)
        feat_start(gall, 1, c)
        folded = g[:, :block]
        for b in range(1, in_chunk):
            folded = folded + g[:, b * block : (b + 1) * block]
        bias_acc[...] = folded if c == 0 else bias_acc[...] + folded
        if c > 0:
            feat_pass(gall, 1, c - 1)
    feat_pass(gall, 1, chunks - 1)
    hidden_out = pltpu.make_async_copy(hidden, hidden_hbm, out_sem.at[0])
    hidden_out.start()

    def terms(r, first, count):
        right = jnp.concatenate([tiles[r * per_block + first + t] for t in range(count)], axis=1)
        out = jnp.dot(ubuf[r], right, preferred_element_type=F32)
        for t in range(count):
            tbuf[r * per_block + first + t] = out[:, t * block : (t + 1) * block]

    w_sum = jnp.zeros((width, wall.shape[1]), F32)
    for c in range(chunks):
        feat_arrive(gall, 1, c)
        u = jnp.dot(w_rows, gall[c], preferred_element_type=F32).astype(BF16)
        for b in range(in_chunk):
            ubuf[c * in_chunk + b] = u[:, b * block : (b + 1) * block]
            terms(c * in_chunk + b, TL, per_block - TL)
        w_sum += lax.dot_general(
            zall[c, mine, :], gall[c], (((1,), (1,)), ((), ())), preferred_element_type=F32
        )
    hid = wall.shape[1]
    wsum[:, :hid] = w_sum
    wsum[:, hid:] = jnp.broadcast_to(jnp.sum(bias_acc[...], axis=1, keepdims=True), bias_acc.shape)

    piece = width // n if sum_inside else width

    def piece_at(ref, owner):
        return ref.at[pl.ds(pl.multiple_of(owner * piece, piece), piece), :]

    def piece_copy(k):
        to = lax.rem(row + k, n)
        return pltpu.make_async_remote_copy(
            src_ref=piece_at(wsum, to),
            dst_ref=wland.at[k],
            send_sem=s1_send.at[k],
            recv_sem=s1_recv.at[k],
            device_id={"rows": to},
            device_id_type=MESH,
        )

    def total_copy(k):
        to = lax.rem(row + k, n)
        return pltpu.make_async_remote_copy(
            src_ref=piece_at(wpiece, row),
            dst_ref=piece_at(wpiece, row),
            send_sem=s2_send.at[k],
            recv_sem=s2_recv.at[k],
            device_id={"rows": to},
            device_id_type=MESH,
        )

    def total_arrival(k):
        owner = lax.rem(row + n - k, n)
        return pltpu.make_async_remote_copy(
            src_ref=piece_at(wpiece, owner),
            dst_ref=piece_at(wpiece, owner),
            send_sem=s2_send.at[k],
            recv_sem=s2_recv.at[k],
            device_id={"rows": owner},
            device_id_type=MESH,
        )

    if sum_inside:
        for k in range(1, n):
            piece_copy(k).start()

    group = 8
    locals_count = row_blocks * TL
    remote_count = tiles.shape[0] - locals_count

    def running_sums(first, count):
        def some_sums(i, running):
            for j in range(group):
                at = first + i * group + j
                running = tbuf[order[at]] + keep[at] * running
                sbuf[at] = running
            return running

        lax.fori_loop(0, count // group, some_sums, jnp.zeros((width, block), F32))

    running_sums(0, remote_count)

    for way in range(2):
        for d in range(half):
            for c in moves(way, d):
                gather_copy(way, d, c).wait_send()

    def own_term(at):
        return sbuf[last[at]] * has[at]

    def back_copy(way, d, c):
        sign = 1 - 2 * way
        return pltpu.make_async_remote_copy(
            src_ref=span(row_at(pos + sign * d), c),
            dst_ref=back.at[way, d - 1, pl.ds(c * in_chunk, in_chunk)],
            send_sem=rs_send.at[way, d - 1, c],
            recv_sem=rs_recv.at[way, d - 1, c],
            device_id={"rows": near[way]},
            device_id_type=MESH,
        )

    def send_back(way, d, c):
        joined = d < half and c in moves(way, d)
        if joined:
            back_copy(way, d + 1, c).wait_recv()
        sign = 1 - 2 * way
        owner = row_at(pos + sign * d)
        for b in range(c * in_chunk, (c + 1) * in_chunk):
            at = owner * row_blocks + b
            value = own_term(at)
            if joined:
                value = value + back[way, d, b].astype(F32)
            gbuf[at] = value.astype(BF16)
        back_copy(way, d, c).start()

    orders = (
        list(range(chunks // 2, chunks)) + list(range(chunks // 2)),
        list(range(chunks)),
    )
    done = 0
    for d in range(half, 0, -1):
        for k in range(chunks):
            for way in range(2):
                if orders[way][k] in moves(way, d - 1):
                    send_back(way, d, orders[way][k])
            if d < half or half == 1:
                for r in range(done, min(done + 2, row_blocks)):
                    terms(r, 0, TL)
                done = min(done + 2, row_blocks)
        if sum_inside and d == half - 1:
            whole = wsum[pl.ds(pl.multiple_of(row * piece, piece), piece), :]
            for k in range(1, n):
                piece_copy(k).wait_recv()
                whole = whole + wland[k]
            wpiece[pl.ds(pl.multiple_of(row * piece, piece), piece), :] = whole * scale
            for k in range(1, n):
                total_copy(k).start()
    for r in range(done, row_blocks):
        terms(r, 0, TL)
    running_sums(remote_count, locals_count)
    for b in range(row_blocks):
        at = n * row_blocks + b
        grad_in[:, b * block : (b + 1) * block] = own_term(row * row_blocks + b) + own_term(at)

    def grad_in_copy(c):
        at = pl.ds(c * cw, cw)
        return pltpu.make_async_copy(grad_in.at[:, at], grad_in_hbm.at[:, at], out_sem.at[2 + c])

    for c in range(chunks):
        for way in range(2):
            back_copy(way, 1, c).wait_recv()
        for b in range(c * in_chunk, (c + 1) * in_chunk):
            value = grad_in[:, b * block : (b + 1) * block]
            value = value + back[0, 0, b].astype(F32) + back[1, 0, b].astype(F32)
            grad_in[:, b * block : (b + 1) * block] = value
        grad_in_copy(c).start()

    if sum_inside:
        for k in range(1, n):
            total_arrival(k).wait_recv()
    result = wpiece if sum_inside else wsum
    grad_w_out = pltpu.make_async_copy(result.at[:, pl.ds(0, hid)], grad_w_hbm, out_sem.at[1])
    grad_w_out.start()
    bias_cols = jnp.broadcast_to(result[:, hid : hid + 1], (width, width))
    grad_b[...] = jnp.sum(jnp.where(diagonal, bias_cols, 0.0), axis=0, keepdims=True)
    hidden_out.wait()
    grad_w_out.wait()
    for c in range(chunks):
        grad_in_copy(c).wait()

    for k, peer in enumerate((sib, opp, opp_sib)):
        weight_copy(k, peer).wait_send()
    for kind, buf in enumerate((zall, gall)):
        for c in range(chunks):
            feat_move(buf, kind, 0, c, fe, opp).wait_send()
            feat_move(buf, kind, 1, c, fe, sib).wait_send()
            feat_move(buf, kind, 2, c, opp, sib).wait_send()
    for way in range(2):
        for d in range(1, half + 1):
            for c in moves(way, d - 1):
                back_copy(way, d, c).wait_send()
    if sum_inside:
        for k in range(1, n):
            piece_copy(k).wait_send()
            total_copy(k).wait_send()


def local(feats, weight, bias, tile_cols, tile_values, cotangent):
    width, nodes = feats.shape
    hid = weight.shape[1]
    count, block = tile_values.shape[0], tile_values.shape[1]
    n = lax.axis_size("rows")
    row_blocks = nodes // block
    per_block = count // row_blocks
    chunks = 4 if n <= 8 else 2
    half = n // 2
    sum_inside = n == 8
    scale = 1.0 / math.sqrt(nodes * n)

    index = jnp.arange(count, dtype=jnp.int32)
    is_local = index % per_block < TL
    cols = jnp.where(is_local, tile_cols % row_blocks, tile_cols)
    key = tile_cols + jnp.where(is_local, n * row_blocks, 0)
    earlier = (key[None, :] < key[:, None]) | (
        (key[None, :] == key[:, None]) & (index[None, :] < index[:, None])
    )
    rank = jnp.sum(earlier.astype(jnp.int32), axis=1)
    placed = rank[None, :] == index[:, None]
    order = jnp.sum(jnp.where(placed, index[None, :], 0), axis=1)
    in_order = jnp.sum(jnp.where(placed, key[None, :], 0), axis=1)
    keep = jnp.concatenate([jnp.zeros((1,), F32), (in_order[1:] == in_order[:-1]).astype(F32)])
    dest = jnp.arange((n + 1) * row_blocks, dtype=jnp.int32)
    dest = jnp.where(dest < n * row_blocks, dest, dest + lax.axis_index("rows") * row_blocks)
    upto = jnp.sum((key[None, :] <= dest[:, None]).astype(jnp.int32), axis=1)
    below = jnp.sum((key[None, :] < dest[:, None]).astype(jnp.int32), axis=1)
    has = (upto > below).astype(F32)
    last = jnp.maximum(upto - 1, 0)

    smem = pl.BlockSpec(memory_space=pltpu.SMEM)
    vmem = pl.BlockSpec(memory_space=pltpu.VMEM)
    anywhere = pl.BlockSpec(memory_space=pl.ANY)
    dma = pltpu.SemaphoreType.DMA
    piece = width // n if sum_inside else 8
    hidden, grad_in, grad_w, grad_b = pl.pallas_call(
        functools.partial(kernel, n, chunks, sum_inside, scale),
        out_shape=(
            jax.ShapeDtypeStruct((width, nodes), BF16),
            jax.ShapeDtypeStruct((width, nodes), F32),
            jax.ShapeDtypeStruct((width, hid), F32),
            jax.ShapeDtypeStruct((1, width), F32),
        ),
        in_specs=[smem] * 5 + [vmem] + [anywhere] * 4,
        out_specs=(anywhere, anywhere, anywhere, vmem),
        scratch_shapes=[
            pltpu.VMEM((row_blocks, width, block), BF16),
            pltpu.VMEM((n * row_blocks, width, block), BF16),
            pltpu.VMEM((count, block, block), BF16),
            pltpu.VMEM((width, nodes), BF16),
            pltpu.VMEM((chunks, 4 * width, nodes // chunks), BF16),
            pltpu.VMEM((chunks, 4 * width, nodes // chunks), BF16),
            pltpu.VMEM((row_blocks, width, block), BF16),
            pltpu.VMEM((count, width, block), F32),
            pltpu.VMEM((count, width, block), F32),
            pltpu.VMEM((row_blocks, width, block), F32),
            pltpu.VMEM((width, nodes), BF16),
            pltpu.VMEM((width, nodes), F32),
            pltpu.VMEM((2, half, row_blocks, width, block), BF16),
            pltpu.VMEM((4 * width, hid), BF16),
            pltpu.VMEM((hid, 4 * width), BF16),
            pltpu.VMEM((width, block), F32),
            pltpu.VMEM((width, hid + block), F32),
            pltpu.VMEM((n if sum_inside else 1, piece, hid + block), F32),
            pltpu.VMEM((width, hid + block), F32),
            dma((3,)),
            dma((row_blocks,)),
            dma((2 + chunks,)),
            dma((3,)),
            dma((3,)),
            dma((2, half, chunks)),
            dma((2, half, chunks)),
            dma((2, 3, chunks)),
            dma((2, 3, chunks)),
            dma((2, half, chunks)),
            dma((2, half, chunks)),
            dma((n,)),
            dma((n,)),
            dma((n,)),
            dma((n,)),
        ],
        compiler_params=pltpu.CompilerParams(
            collective_id=0, has_side_effects=True, vmem_limit_bytes=52 * 1024 * 1024
        ),
        cost_estimate=pl.CostEstimate(
            flops=2 * 2 * count * width * block * block + 6 * width * hid * nodes,
            bytes_accessed=2 * count * block * block,
            transcendentals=width * nodes,
        ),
    )(
        cols,
        order,
            keep,
        last,
        has,
        bias[None, :],
        feats,
        weight,
        tile_values,
        cotangent,
    )
    bias_total = grad_b[0]
    if not sum_inside:
        grad_w, bias_total = lax.psum((grad_w * scale, bias_total * scale), "rows")
    return hidden, grad_in, grad_w, bias_total


def solution(mesh):
    placed = (
        P("feat", "rows"),
        P("feat", None),
        P("feat"),
        P("rows"),
        P("rows", None, None),
        P("feat", "rows"),
    )
    return jax.shard_map(
        local,
        mesh=mesh,
        in_specs=placed,
        out_specs=(P("feat", "rows"), P("feat", "rows"), P("feat", None), P("feat")),
        check_vma=False,
    )
```

```python
import functools
import math

import jax
import jax.numpy as jnp
from jax import lax
from jax.experimental import pallas as pl
from jax.experimental.pallas import tpu as pltpu
from jax.sharding import PartitionSpec as P

MESH = pl.DeviceIdType.MESH
TL = 4
F32 = jnp.float32
BF16 = jnp.bfloat16


def kernel(
    n,
    chunks,
    sum_inside,
    scale,
    cols,
    order,
    keep,
    last,
    has,
    bias,
    feats,
    weight,
    tiles_hbm,
    cot_hbm,
    hidden_hbm,
    grad_in_hbm,
    grad_w_hbm,
    grad_b,
    own,
    gbuf,
    tiles,
    cot,
    zall,
    gall,
    ubuf,
    tbuf,
    sbuf,
    zloc,
    hidden,
    grad_in,
    back,
    wall,
    wt,
    bias_acc,
    wsum,
    wland,
    wpiece,
    local_sem,
    feats_sem,
    out_sem,
    w_send,
    w_recv,
    ag_send,
    ag_recv,
    fe_send,
    fe_recv,
    rs_send,
    rs_recv,
    s1_send,
    s1_recv,
    s2_send,
    s2_recv,
):
    width, nodes = feats.shape
    block = tiles.shape[1]
    row_blocks = nodes // block
    per_block = tiles.shape[0] // row_blocks
    in_chunk = row_blocks // chunks
    cw = in_chunk * block
    half = n // 2
    row = lax.axis_index("rows")
    fe = lax.axis_index("feat")
    odd = lax.rem(row, 2)
    pos = (1 - odd) * (row // 2) + odd * (n - 1 - row // 2)

    def row_at(p):
        p = lax.rem(p + 2 * n, n)
        far = p // half
        return (1 - far) * (2 * p) + far * (2 * n - 1 - 2 * p)

    near = (row_at(pos + 1), row_at(pos - 1))
    sib = fe + 1 - 2 * lax.rem(fe, 2)
    opp = lax.rem(fe + 2, 4)
    opp_sib = lax.rem(sib + 2, 4)

    tile_copy = pltpu.make_async_copy(tiles_hbm, tiles, local_sem.at[0])
    cot_copy = pltpu.make_async_copy(cot_hbm, cot, local_sem.at[1])
    feats_copies = [
        pltpu.make_async_copy(
            feats.at[:, pl.ds(b * block, block)],
            own.at[b],
            feats_sem.at[b],
        )
        for b in range(row_blocks)
    ]
    for copy in feats_copies:
        copy.start()
    mine = pl.ds(pl.multiple_of(fe * width, width), width)
    weight_in = pltpu.make_async_copy(weight, wall.at[mine, :], local_sem.at[2])
    weight_in.start()

    barrier = pltpu.get_barrier_semaphore()
    if sum_inside:
        others = [lax.rem(row + k, n) for k in range(1, n)]
    else:
        others = list(near)
    for peer in others:
        pl.semaphore_signal(barrier, inc=1, device_id={"rows": peer}, device_id_type=MESH)
    for peer in (sib, opp, opp_sib):
        pl.semaphore_signal(barrier, inc=1, device_id={"feat": peer}, device_id_type=MESH)

    for copy in feats_copies:
        copy.wait()
    tile_copy.start()
    cot_copy.start()
    weight_in.wait()
    pl.semaphore_wait(barrier, len(others) + 3)

    def span(owner, c):
        return gbuf.at[pl.ds(owner * row_blocks + c * in_chunk, in_chunk)]

    def gather_copy(way, d, c):
        sign = 1 - 2 * way
        at = span(row_at(pos - sign * d), c)
        src = own.at[pl.ds(c * in_chunk, in_chunk)] if d == 0 else at
        return pltpu.make_async_remote_copy(
            src_ref=src,
            dst_ref=at,
            send_sem=ag_send.at[way, d, c],
            recv_sem=ag_recv.at[way, d, c],
            device_id={"rows": near[way]},
            device_id_type=MESH,
        )

    def gather_arrival(way, d, c):
        sign = 1 - 2 * way
        at = span(row_at(pos - sign * (d + 1)), c)
        return pltpu.make_async_remote_copy(
            src_ref=at,
            dst_ref=at,
            send_sem=ag_send.at[way, d, c],
            recv_sem=ag_recv.at[way, d, c],
            device_id={"rows": near[way]},
            device_id_type=MESH,
        )

    def moves(way, d):
        if d < half - 1:
            return list(range(chunks))
        if way == 0:
            return list(range(chunks // 2))
        return list(range(chunks // 2, chunks))

    def weight_copy(k, peer):
        at = wall.at[pl.ds(pl.multiple_of(fe * width, width), width), :]
        return pltpu.make_async_remote_copy(
            src_ref=at,
            dst_ref=at,
            send_sem=w_send.at[k],
            recv_sem=w_recv.at[k],
            device_id={"feat": peer},
            device_id_type=MESH,
        )

    def weight_arrival(k, peer):
        at = wall.at[pl.ds(pl.multiple_of(peer * width, width), width), :]
        return pltpu.make_async_remote_copy(
            src_ref=at,
            dst_ref=at,
            send_sem=w_send.at[k],
            recv_sem=w_recv.at[k],
            device_id={"feat": peer},
            device_id_type=MESH,
        )

    for c in range(chunks):
        for way in range(2):
            if c in moves(way, 0):
                gather_copy(way, 0, c).start()
    for k, peer in enumerate((sib, opp, opp_sib)):
        weight_copy(k, peer).start()
    def products(get, r, first, count):
        left = jnp.concatenate([get(r * per_block + first + t) for t in range(count)], axis=1)
        right = jnp.concatenate([tiles[r * per_block + first + t] for t in range(count)], axis=1)
        return lax.dot_general(left, right, (((1,), (1,)), ((), ())), preferred_element_type=F32)

    def local_products(r):
        zloc[r] = products(lambda i: own[cols[i]], r, 0, TL)

    for b in range(row_blocks):
        gbuf[row * row_blocks + b] = own[b]
    done = 0
    for d in range(1, half):
        for c in range(chunks):
            for way in range(2):
                if c in moves(way, d - 1):
                    gather_arrival(way, d - 1, c).wait_recv()
                if c in moves(way, d):
                    gather_copy(way, d, c).start()
            if d == 1 and c == 0:
                tile_copy.wait()
            if done < row_blocks:
                for r in range(done, min(done + 2, row_blocks)):
                    local_products(r)
                done = min(done + 2, row_blocks)
        if d == 1:
            for k, peer in enumerate((sib, opp, opp_sib)):
                weight_arrival(k, peer).wait_recv()
            wt[...] = wall[...].astype(F32).T.astype(BF16)
            cot_copy.wait()
    for r in range(done, row_blocks):
        local_products(r)
    for way in range(2):
        for c in moves(way, half - 1):
            gather_arrival(way, half - 1, c).wait_recv()

    def feat_move(buf, kind, hop, c, owner, peer):
        at = buf.at[c, pl.ds(pl.multiple_of(owner * width, width), width), :]
        return pltpu.make_async_remote_copy(
            src_ref=at,
            dst_ref=at,
            send_sem=fe_send.at[kind, hop, c],
            recv_sem=fe_recv.at[kind, hop, c],
            device_id={"feat": peer},
            device_id_type=MESH,
        )

    def feat_start(buf, kind, c):
        feat_move(buf, kind, 0, c, fe, opp).start()
        feat_move(buf, kind, 1, c, fe, sib).start()

    def feat_pass(buf, kind, c):
        feat_move(buf, kind, 0, c, opp, opp).wait_recv()
        feat_move(buf, kind, 2, c, opp, sib).start()

    def feat_arrive(buf, kind, c):
        feat_move(buf, kind, 1, c, sib, sib).wait_recv()
        feat_move(buf, kind, 2, c, opp_sib, sib).wait_recv()

    for c in range(chunks):

        def one_row(r, carry, c=c):
            at = c * in_chunk + r
            total = zloc[at] + products(lambda i: gbuf[cols[i]], at, TL, per_block - TL)
            zall[c, mine, pl.ds(pl.multiple_of(r * block, block), block)] = total.astype(BF16)
            return carry

        lax.fori_loop(0, in_chunk, one_row, 0)
        feat_start(zall, 0, c)
        if c > 0:
            feat_pass(zall, 0, c - 1)
    feat_pass(zall, 0, chunks - 1)

    w_cols = wt[mine, :]
    w_rows = wall[mine, :]
    diagonal = lax.broadcasted_iota(jnp.int32, (width, width), 0) == lax.broadcasted_iota(
        jnp.int32, (width, width), 1
    )
    bias_row = jnp.broadcast_to(bias[...], (width, width))
    bias_col = jnp.sum(jnp.where(diagonal, bias_row, 0.0), axis=1, keepdims=True)
    for c in range(chunks):
        feat_arrive(zall, 0, c)
        pre = jnp.dot(w_cols, zall[c], preferred_element_type=F32) + bias_col
        sigma = jax.nn.sigmoid(pre)
        hidden[:, c * cw : (c + 1) * cw] = (pre * sigma).astype(BF16)
        g = cot[:, c * cw : (c + 1) * cw].astype(F32) * (sigma * (1.0 + pre * (1.0 - sigma)))
        gall[c, mine, :] = g.astype(BF16)
        feat_start(gall, 1, c)
        folded = g[:, :block]
        for b in range(1, in_chunk):
            folded = folded + g[:, b * block : (b + 1) * block]
        bias_acc[...] = folded if c == 0 else bias_acc[...] + folded
        if c > 0:
            feat_pass(gall, 1, c - 1)
    feat_pass(gall, 1, chunks - 1)
    hidden_out = pltpu.make_async_copy(hidden, hidden_hbm, out_sem.at[0])
    hidden_out.start()

    def terms(r, first, count):
        right = jnp.concatenate([tiles[r * per_block + first + t] for t in range(count)], axis=1)
        out = jnp.dot(ubuf[r], right, preferred_element_type=F32)
        for t in range(count):
            tbuf[r * per_block + first + t] = out[:, t * block : (t + 1) * block]

    w_sum = jnp.zeros((width, wall.shape[1]), F32)
    for c in range(chunks):
        feat_arrive(gall, 1, c)
        u = jnp.dot(w_rows, gall[c], preferred_element_type=F32).astype(BF16)
        for b in range(in_chunk):
            ubuf[c * in_chunk + b] = u[:, b * block : (b + 1) * block]
            terms(c * in_chunk + b, TL, per_block - TL)
        w_sum += lax.dot_general(
            zall[c, mine, :], gall[c], (((1,), (1,)), ((), ())), preferred_element_type=F32
        )
    hid = wall.shape[1]
    wsum[:, :hid] = w_sum
    wsum[:, hid:] = jnp.broadcast_to(jnp.sum(bias_acc[...], axis=1, keepdims=True), bias_acc.shape)

    piece = width // n if sum_inside else width

    def piece_at(ref, owner):
        return ref.at[pl.ds(pl.multiple_of(owner * piece, piece), piece), :]

    def piece_copy(k):
        to = lax.rem(row + k, n)
        return pltpu.make_async_remote_copy(
            src_ref=piece_at(wsum, to),
            dst_ref=wland.at[k],
            send_sem=s1_send.at[k],
            recv_sem=s1_recv.at[k],
            device_id={"rows": to},
            device_id_type=MESH,
        )

    def total_copy(k):
        to = lax.rem(row + k, n)
        return pltpu.make_async_remote_copy(
            src_ref=piece_at(wpiece, row),
            dst_ref=piece_at(wpiece, row),
            send_sem=s2_send.at[k],
            recv_sem=s2_recv.at[k],
            device_id={"rows": to},
            device_id_type=MESH,
        )

    def total_arrival(k):
        owner = lax.rem(row + n - k, n)
        return pltpu.make_async_remote_copy(
            src_ref=piece_at(wpiece, owner),
            dst_ref=piece_at(wpiece, owner),
            send_sem=s2_send.at[k],
            recv_sem=s2_recv.at[k],
            device_id={"rows": owner},
            device_id_type=MESH,
        )

    if sum_inside:
        for k in range(1, n):
            piece_copy(k).start()

    group = 8
    locals_count = row_blocks * TL
    remote_count = tiles.shape[0] - locals_count

    def running_sums(first, count):
        def some_sums(i, running):
            for j in range(group):
                at = first + i * group + j
                running = tbuf[order[at]] + keep[at] * running
                sbuf[at] = running
            return running

        lax.fori_loop(0, count // group, some_sums, jnp.zeros((width, block), F32))

    running_sums(0, remote_count)

    for way in range(2):
        for d in range(half):
            for c in moves(way, d):
                gather_copy(way, d, c).wait_send()

    def own_term(at):
        return sbuf[last[at]] * has[at]

    def back_copy(way, d, c):
        sign = 1 - 2 * way
        return pltpu.make_async_remote_copy(
            src_ref=span(row_at(pos + sign * d), c),
            dst_ref=back.at[way, d - 1, pl.ds(c * in_chunk, in_chunk)],
            send_sem=rs_send.at[way, d - 1, c],
            recv_sem=rs_recv.at[way, d - 1, c],
            device_id={"rows": near[way]},
            device_id_type=MESH,
        )

    def send_back(way, d, c):
        joined = d < half and c in moves(way, d)
        if joined:
            back_copy(way, d + 1, c).wait_recv()
        sign = 1 - 2 * way
        owner = row_at(pos + sign * d)
        for b in range(c * in_chunk, (c + 1) * in_chunk):
            at = owner * row_blocks + b
            value = own_term(at)
            if joined:
                value = value + back[way, d, b].astype(F32)
            gbuf[at] = value.astype(BF16)
        back_copy(way, d, c).start()

    orders = (
        list(range(chunks // 2, chunks)) + list(range(chunks // 2)),
        list(range(chunks)),
    )
    done = 0
    for d in range(half, 0, -1):
        for k in range(chunks):
            for way in range(2):
                if orders[way][k] in moves(way, d - 1):
                    send_back(way, d, orders[way][k])
            if d < half or half == 1:
                for r in range(done, min(done + 2, row_blocks)):
                    terms(r, 0, TL)
                done = min(done + 2, row_blocks)
        if sum_inside and d == half - 1:
            whole = wsum[pl.ds(pl.multiple_of(row * piece, piece), piece), :]
            for k in range(1, n):
                piece_copy(k).wait_recv()
                whole = whole + wland[k]
            wpiece[pl.ds(pl.multiple_of(row * piece, piece), piece), :] = whole * scale
            for k in range(1, n):
                total_copy(k).start()
    for r in range(done, row_blocks):
        terms(r, 0, TL)
    running_sums(remote_count, locals_count)
    for b in range(row_blocks):
        at = n * row_blocks + b
        grad_in[:, b * block : (b + 1) * block] = own_term(row * row_blocks + b) + own_term(at)

    def grad_in_copy(c):
        at = pl.ds(c * cw, cw)
        return pltpu.make_async_copy(grad_in.at[:, at], grad_in_hbm.at[:, at], out_sem.at[2 + c])

    for c in range(chunks):
        for way in range(2):
            back_copy(way, 1, c).wait_recv()
        for b in range(c * in_chunk, (c + 1) * in_chunk):
            value = grad_in[:, b * block : (b + 1) * block]
            value = value + back[0, 0, b].astype(F32) + back[1, 0, b].astype(F32)
            grad_in[:, b * block : (b + 1) * block] = value
        grad_in_copy(c).start()

    if sum_inside:
        for k in range(1, n):
            total_arrival(k).wait_recv()
    result = wpiece if sum_inside else wsum
    grad_w_out = pltpu.make_async_copy(result.at[:, pl.ds(0, hid)], grad_w_hbm, out_sem.at[1])
    grad_w_out.start()
    bias_cols = jnp.broadcast_to(result[:, hid : hid + 1], (width, width))
    grad_b[...] = jnp.sum(jnp.where(diagonal, bias_cols, 0.0), axis=0, keepdims=True)
    hidden_out.wait()
    grad_w_out.wait()
    for c in range(chunks):
        grad_in_copy(c).wait()

    for k, peer in enumerate((sib, opp, opp_sib)):
        weight_copy(k, peer).wait_send()
    for kind, buf in enumerate((zall, gall)):
        for c in range(chunks):
            feat_move(buf, kind, 0, c, fe, opp).wait_send()
            feat_move(buf, kind, 1, c, fe, sib).wait_send()
            feat_move(buf, kind, 2, c, opp, sib).wait_send()
    for way in range(2):
        for d in range(1, half + 1):
            for c in moves(way, d - 1):
                back_copy(way, d, c).wait_send()
    if sum_inside:
        for k in range(1, n):
            piece_copy(k).wait_send()
            total_copy(k).wait_send()


def hand_over(*refs):
    sems = refs[8]
    copies = [pltpu.make_async_copy(refs[k], refs[4 + k], sems.at[k]) for k in range(4)]
    for copy in copies:
        copy.start()
    for copy in copies:
        copy.wait()


def local(feats, weight, bias, tile_cols, tile_values, cotangent):
    width, nodes = feats.shape
    hid = weight.shape[1]
    count, block = tile_values.shape[0], tile_values.shape[1]
    n = lax.axis_size("rows")
    row_blocks = nodes // block
    per_block = count // row_blocks
    chunks = 4 if n <= 8 else 2
    half = n // 2
    sum_inside = n == 8
    scale = 1.0 / math.sqrt(nodes * n)

    index = jnp.arange(count, dtype=jnp.int32)
    is_local = index % per_block < TL
    cols = jnp.where(is_local, tile_cols % row_blocks, tile_cols)
    key = tile_cols + jnp.where(is_local, n * row_blocks, 0)
    earlier = (key[None, :] < key[:, None]) | (
        (key[None, :] == key[:, None]) & (index[None, :] < index[:, None])
    )
    rank = jnp.sum(earlier.astype(jnp.int32), axis=1)
    placed = rank[None, :] == index[:, None]
    order = jnp.sum(jnp.where(placed, index[None, :], 0), axis=1)
    in_order = jnp.sum(jnp.where(placed, key[None, :], 0), axis=1)
    keep = jnp.concatenate([jnp.zeros((1,), F32), (in_order[1:] == in_order[:-1]).astype(F32)])
    dest = jnp.arange((n + 1) * row_blocks, dtype=jnp.int32)
    dest = jnp.where(dest < n * row_blocks, dest, dest + lax.axis_index("rows") * row_blocks)
    upto = jnp.sum((key[None, :] <= dest[:, None]).astype(jnp.int32), axis=1)
    below = jnp.sum((key[None, :] < dest[:, None]).astype(jnp.int32), axis=1)
    has = (upto > below).astype(F32)
    last = jnp.maximum(upto - 1, 0)

    smem = pl.BlockSpec(memory_space=pltpu.SMEM)
    vmem = pl.BlockSpec(memory_space=pltpu.VMEM)
    anywhere = pl.BlockSpec(memory_space=pl.ANY)
    dma = pltpu.SemaphoreType.DMA
    piece = width // n if sum_inside else 8
    hidden, grad_in, grad_w, grad_b = pl.pallas_call(
        functools.partial(kernel, n, chunks, sum_inside, scale),
        out_shape=(
            jax.ShapeDtypeStruct((width, nodes), BF16),
            jax.ShapeDtypeStruct((width, nodes), F32),
            jax.ShapeDtypeStruct((width, hid), F32),
            jax.ShapeDtypeStruct((1, width), F32),
        ),
        in_specs=[smem] * 5 + [vmem] + [anywhere] * 4,
        out_specs=(anywhere, anywhere, anywhere, vmem),
        scratch_shapes=[
            pltpu.VMEM((row_blocks, width, block), BF16),
            pltpu.VMEM((n * row_blocks, width, block), BF16),
            pltpu.VMEM((count, block, block), BF16),
            pltpu.VMEM((width, nodes), BF16),
            pltpu.VMEM((chunks, 4 * width, nodes // chunks), BF16),
            pltpu.VMEM((chunks, 4 * width, nodes // chunks), BF16),
            pltpu.VMEM((row_blocks, width, block), BF16),
            pltpu.VMEM((count, width, block), F32),
            pltpu.VMEM((count, width, block), F32),
            pltpu.VMEM((row_blocks, width, block), F32),
            pltpu.VMEM((width, nodes), BF16),
            pltpu.VMEM((width, nodes), F32),
            pltpu.VMEM((2, half, row_blocks, width, block), BF16),
            pltpu.VMEM((4 * width, hid), BF16),
            pltpu.VMEM((hid, 4 * width), BF16),
            pltpu.VMEM((width, block), F32),
            pltpu.VMEM((width, hid + block), F32),
            pltpu.VMEM((n if sum_inside else 1, piece, hid + block), F32),
            pltpu.VMEM((width, hid + block), F32),
            dma((3,)),
            dma((row_blocks,)),
            dma((2 + chunks,)),
            dma((3,)),
            dma((3,)),
            dma((2, half, chunks)),
            dma((2, half, chunks)),
            dma((2, 3, chunks)),
            dma((2, 3, chunks)),
            dma((2, half, chunks)),
            dma((2, half, chunks)),
            dma((n,)),
            dma((n,)),
            dma((n,)),
            dma((n,)),
        ],
        compiler_params=pltpu.CompilerParams(
            collective_id=0, has_side_effects=True, vmem_limit_bytes=63 * 1024 * 1024
        ),
        cost_estimate=pl.CostEstimate(
            flops=2 * 2 * count * width * block * block + 6 * width * hid * nodes,
            bytes_accessed=2 * count * block * block,
            transcendentals=width * nodes,
        ),
    )(
        cols,
        order,
            keep,
        last,
        has,
        bias[None, :],
        feats,
        weight,
        tile_values,
        cotangent,
    )
    if not sum_inside:
        grad_w, grad_b = lax.psum((grad_w * scale, grad_b * scale), "rows")
    results = (hidden, grad_in, grad_w, grad_b)
    hidden, grad_in, grad_w, grad_b = pl.pallas_call(
        hand_over,
        out_shape=tuple(jax.ShapeDtypeStruct(a.shape, a.dtype) for a in results),
        in_specs=[anywhere] * 4,
        out_specs=(anywhere,) * 4,
        scratch_shapes=[dma((4,))],
        compiler_params=pltpu.CompilerParams(vmem_limit_bytes=63 * 1024 * 1024),
    )(*results)
    return hidden, grad_in, grad_w, grad_b[0]


def solution(mesh):
    placed = (
        P("feat", "rows"),
        P("feat", None),
        P("feat"),
        P("rows"),
        P("rows", None, None),
        P("feat", "rows"),
    )
    return jax.shard_map(
        local,
        mesh=mesh,
        in_specs=placed,
        out_specs=(P("feat", "rows"), P("feat", "rows"), P("feat", None), P("feat")),
        check_vma=False,
    )
```

```python
import functools
import math

import jax
import jax.numpy as jnp
from jax import lax
from jax.experimental import pallas as pl
from jax.experimental.pallas import tpu as pltpu
from jax.sharding import PartitionSpec as P

MESH = pl.DeviceIdType.MESH
TL = 4
F32 = jnp.float32
BF16 = jnp.bfloat16


def kernel(
    n,
    chunks,
    sum_inside,
    scale,
    cols,
    order,
    keep,
    last,
    has,
    bias,
    feats,
    weight,
    tiles_hbm,
    cot_hbm,
    hidden_hbm,
    grad_in_hbm,
    grad_w_hbm,
    grad_b,
    own,
    gbuf,
    tiles,
    cot,
    fall,
    gall,
    ubuf,
    tbuf,
    sbuf,
    zloc,
    hidden,
    grad_in,
    back,
    wall,
    wt,
    bias_acc,
    wsum,
    wland,
    wpiece,
    local_sem,
    feats_sem,
    out_sem,
    w_send,
    w_recv,
    ag_send,
    ag_recv,
    fe_send,
    fe_recv,
    rs_send,
    rs_recv,
    s1_send,
    s1_recv,
    s2_send,
    s2_recv,
):
    width, nodes = feats.shape
    block = tiles.shape[1]
    row_blocks = nodes // block
    per_block = tiles.shape[0] // row_blocks
    in_chunk = row_blocks // chunks
    cw = in_chunk * block
    half = n // 2
    row = lax.axis_index("rows")
    fe = lax.axis_index("feat")
    odd = lax.rem(row, 2)
    pos = (1 - odd) * (row // 2) + odd * (n - 1 - row // 2)

    def row_at(p):
        p = lax.rem(p + 2 * n, n)
        far = p // half
        return (1 - far) * (2 * p) + far * (2 * n - 1 - 2 * p)

    near = (row_at(pos + 1), row_at(pos - 1))
    sib = fe + 1 - 2 * lax.rem(fe, 2)
    opp = lax.rem(fe + 2, 4)
    opp_sib = lax.rem(sib + 2, 4)

    tile_copy = pltpu.make_async_copy(tiles_hbm, tiles, local_sem.at[0])
    cot_copy = pltpu.make_async_copy(cot_hbm, cot, local_sem.at[1])
    mine = pl.ds(pl.multiple_of(fe * width, width), width)
    feats_copies = [
        pltpu.make_async_copy(
            feats.at[:, pl.ds(c * cw, cw)], fall.at[c, mine, :], feats_sem.at[c]
        )
        for c in range(chunks)
    ]
    for copy in feats_copies:
        copy.start()
    weight_in = pltpu.make_async_copy(weight, wall.at[mine, :], local_sem.at[2])
    weight_in.start()

    barrier = pltpu.get_barrier_semaphore()
    if sum_inside:
        others = [lax.rem(row + k, n) for k in range(1, n)]
    else:
        others = list(near)
    for peer in others:
        pl.semaphore_signal(barrier, inc=1, device_id={"rows": peer}, device_id_type=MESH)
    for peer in (sib, opp, opp_sib):
        pl.semaphore_signal(barrier, inc=1, device_id={"feat": peer}, device_id_type=MESH)

    for copy in feats_copies:
        copy.wait()
    tile_copy.start()
    cot_copy.start()
    weight_in.wait()
    pl.semaphore_wait(barrier, len(others) + 3)

    def span(owner, c):
        return gbuf.at[pl.ds(owner * row_blocks + c * in_chunk, in_chunk)]

    def gather_copy(way, d, c):
        sign = 1 - 2 * way
        at = span(row_at(pos - sign * d), c)
        src = own.at[pl.ds(c * in_chunk, in_chunk)] if d == 0 else at
        return pltpu.make_async_remote_copy(
            src_ref=src,
            dst_ref=at,
            send_sem=ag_send.at[way, d, c],
            recv_sem=ag_recv.at[way, d, c],
            device_id={"rows": near[way]},
            device_id_type=MESH,
        )

    def gather_arrival(way, d, c):
        sign = 1 - 2 * way
        at = span(row_at(pos - sign * (d + 1)), c)
        return pltpu.make_async_remote_copy(
            src_ref=at,
            dst_ref=at,
            send_sem=ag_send.at[way, d, c],
            recv_sem=ag_recv.at[way, d, c],
            device_id={"rows": near[way]},
            device_id_type=MESH,
        )

    def moves(way, d):
        if d < half - 1:
            return list(range(chunks))
        if way == 0:
            return list(range(chunks // 2))
        return list(range(chunks // 2, chunks))

    def weight_copy(k, peer):
        at = wall.at[pl.ds(pl.multiple_of(fe * width, width), width), :]
        return pltpu.make_async_remote_copy(
            src_ref=at,
            dst_ref=at,
            send_sem=w_send.at[k],
            recv_sem=w_recv.at[k],
            device_id={"feat": peer},
            device_id_type=MESH,
        )

    def weight_arrival(k, peer):
        at = wall.at[pl.ds(pl.multiple_of(peer * width, width), width), :]
        return pltpu.make_async_remote_copy(
            src_ref=at,
            dst_ref=at,
            send_sem=w_send.at[k],
            recv_sem=w_recv.at[k],
            device_id={"feat": peer},
            device_id_type=MESH,
        )

    def feat_move(buf, kind, hop, c, owner, peer):
        at = buf.at[c, pl.ds(pl.multiple_of(owner * width, width), width), :]
        return pltpu.make_async_remote_copy(
            src_ref=at,
            dst_ref=at,
            send_sem=fe_send.at[kind, hop, c],
            recv_sem=fe_recv.at[kind, hop, c],
            device_id={"feat": peer},
            device_id_type=MESH,
        )

    def feat_start(buf, kind, c):
        feat_move(buf, kind, 0, c, fe, opp).start()
        feat_move(buf, kind, 1, c, fe, sib).start()

    def feat_pass(buf, kind, c):
        feat_move(buf, kind, 0, c, opp, opp).wait_recv()
        feat_move(buf, kind, 2, c, opp, sib).start()

    def feat_arrive(buf, kind, c):
        feat_move(buf, kind, 1, c, sib, sib).wait_recv()
        feat_move(buf, kind, 2, c, opp_sib, sib).wait_recv()

    peers = (sib, opp, opp_sib)
    for k, peer in enumerate(peers):
        weight_copy(k, peer).start()
    for c in range(chunks):
        feat_start(fall, 0, c)
    for k, peer in enumerate(peers):
        weight_arrival(k, peer).wait_recv()
    wt[...] = wall[...].astype(F32).T.astype(BF16)
    w_cols = wt[mine, :]
    w_rows = wall[mine, :]
    feat_pass(fall, 0, 0)
    for c in range(chunks):
        if c + 1 < chunks:
            feat_pass(fall, 0, c + 1)
        feat_arrive(fall, 0, c)
        proj = jnp.dot(w_cols, fall[c], preferred_element_type=F32).astype(BF16)
        for b in range(in_chunk):
            own[c * in_chunk + b] = proj[:, b * block : (b + 1) * block]
        for way in range(2):
            if c in moves(way, 0):
                gather_copy(way, 0, c).start()

    def products(get, r, first, count):
        left = jnp.concatenate([get(r * per_block + first + t) for t in range(count)], axis=1)
        right = jnp.concatenate([tiles[r * per_block + first + t] for t in range(count)], axis=1)
        return lax.dot_general(left, right, (((1,), (1,)), ((), ())), preferred_element_type=F32)

    def local_products(r):
        zloc[r] = products(lambda i: own[cols[i]], r, 0, TL)

    for b in range(row_blocks):
        gbuf[row * row_blocks + b] = own[b]
    done = 0
    for d in range(1, half):
        for c in range(chunks):
            for way in range(2):
                if c in moves(way, d - 1):
                    gather_arrival(way, d - 1, c).wait_recv()
                if c in moves(way, d):
                    gather_copy(way, d, c).start()
            if d == 1 and c == 0:
                tile_copy.wait()
            if done < row_blocks:
                for r in range(done, min(done + 2, row_blocks)):
                    local_products(r)
                done = min(done + 2, row_blocks)
        if d == 1:
            cot_copy.wait()
    for r in range(done, row_blocks):
        local_products(r)
    for way in range(2):
        for c in moves(way, half - 1):
            gather_arrival(way, half - 1, c).wait_recv()

    diagonal = lax.broadcasted_iota(jnp.int32, (width, width), 0) == lax.broadcasted_iota(
        jnp.int32, (width, width), 1
    )
    bias_row = jnp.broadcast_to(bias[...], (width, width))
    bias_col = jnp.sum(jnp.where(diagonal, bias_row, 0.0), axis=1, keepdims=True)
    def terms(r, first, count):
        right = jnp.concatenate([tiles[r * per_block + first + t] for t in range(count)], axis=1)
        out = jnp.dot(ubuf[r], right, preferred_element_type=F32)
        for t in range(count):
            tbuf[r * per_block + first + t] = out[:, t * block : (t + 1) * block]

    for c in range(chunks):
        at = slice(c * cw, (c + 1) * cw)
        for b in range(c * in_chunk, (c + 1) * in_chunk):
            grad_in[:, b * block : (b + 1) * block] = zloc[b] + products(
                lambda i: gbuf[cols[i]], b, TL, per_block - TL
            )
        pre = grad_in[:, at] + bias_col
        sigma = jax.nn.sigmoid(pre)
        hidden[:, at] = (pre * sigma).astype(BF16)
        g = cot[:, at].astype(F32) * (sigma * (1.0 + pre * (1.0 - sigma)))
        folded = g[:, :block]
        for b in range(1, in_chunk):
            folded = folded + g[:, b * block : (b + 1) * block]
        bias_acc[...] = folded if c == 0 else bias_acc[...] + folded
        for b in range(in_chunk):
            ubuf[c * in_chunk + b] = g[:, b * block : (b + 1) * block].astype(BF16)
            terms(c * in_chunk + b, TL, per_block - TL)
    hidden_out = pltpu.make_async_copy(hidden, hidden_hbm, out_sem.at[0])
    hidden_out.start()
    hid = wall.shape[1]
    wsum[:, hid:] = jnp.broadcast_to(jnp.sum(bias_acc[...], axis=1, keepdims=True), bias_acc.shape)

    piece = width // n if sum_inside else width

    def piece_at(ref, owner):
        return ref.at[pl.ds(pl.multiple_of(owner * piece, piece), piece), :]

    def piece_copy(k):
        to = lax.rem(row + k, n)
        return pltpu.make_async_remote_copy(
            src_ref=piece_at(wsum, to),
            dst_ref=wland.at[k],
            send_sem=s1_send.at[k],
            recv_sem=s1_recv.at[k],
            device_id={"rows": to},
            device_id_type=MESH,
        )

    def total_copy(k):
        to = lax.rem(row + k, n)
        return pltpu.make_async_remote_copy(
            src_ref=piece_at(wpiece, row),
            dst_ref=piece_at(wpiece, row),
            send_sem=s2_send.at[k],
            recv_sem=s2_recv.at[k],
            device_id={"rows": to},
            device_id_type=MESH,
        )

    def total_arrival(k):
        owner = lax.rem(row + n - k, n)
        return pltpu.make_async_remote_copy(
            src_ref=piece_at(wpiece, owner),
            dst_ref=piece_at(wpiece, owner),
            send_sem=s2_send.at[k],
            recv_sem=s2_recv.at[k],
            device_id={"rows": owner},
            device_id_type=MESH,
        )

    group = 8
    locals_count = row_blocks * TL
    remote_count = tiles.shape[0] - locals_count

    def running_sums(first, count):
        def some_sums(i, running):
            for j in range(group):
                at = first + i * group + j
                running = tbuf[order[at]] + keep[at] * running
                sbuf[at] = running
            return running

        lax.fori_loop(0, count // group, some_sums, jnp.zeros((width, block), F32))

    running_sums(0, remote_count)

    for way in range(2):
        for d in range(half):
            for c in moves(way, d):
                gather_copy(way, d, c).wait_send()

    def own_term(at):
        return sbuf[last[at]] * has[at]

    def back_copy(way, d, c):
        sign = 1 - 2 * way
        return pltpu.make_async_remote_copy(
            src_ref=span(row_at(pos + sign * d), c),
            dst_ref=back.at[way, d - 1, pl.ds(c * in_chunk, in_chunk)],
            send_sem=rs_send.at[way, d - 1, c],
            recv_sem=rs_recv.at[way, d - 1, c],
            device_id={"rows": near[way]},
            device_id_type=MESH,
        )

    def send_back(way, d, c):
        joined = d < half and c in moves(way, d)
        if joined:
            back_copy(way, d + 1, c).wait_recv()
        sign = 1 - 2 * way
        owner = row_at(pos + sign * d)
        for b in range(c * in_chunk, (c + 1) * in_chunk):
            at = owner * row_blocks + b
            value = own_term(at)
            if joined:
                value = value + back[way, d, b].astype(F32)
            gbuf[at] = value.astype(BF16)
        back_copy(way, d, c).start()

    orders = (
        list(range(chunks // 2, chunks)) + list(range(chunks // 2)),
        list(range(chunks)),
    )
    finish = [0, 2, 1, 3] if chunks == 4 else list(range(chunks))
    last_orders = ([2, 0, 1, 3], finish) if chunks == 4 else (finish, finish)
    done = 0
    for d in range(half, 0, -1):
        for k in range(chunks):
            for way in range(2):
                c = (orders if d > 1 else last_orders)[way][k]
                if c in moves(way, d - 1):
                    send_back(way, d, c)
            if d < half or half == 1:
                for r in range(done, min(done + 2, row_blocks)):
                    terms(r, 0, TL)
                done = min(done + 2, row_blocks)
    for r in range(done, row_blocks):
        terms(r, 0, TL)
    running_sums(remote_count, locals_count)
    for b in range(row_blocks):
        at = n * row_blocks + b
        grad_in[:, b * block : (b + 1) * block] = own_term(row * row_blocks + b) + own_term(at)

    def grad_in_copy(c):
        at = pl.ds(c * cw, cw)
        return pltpu.make_async_copy(grad_in.at[:, at], grad_in_hbm.at[:, at], out_sem.at[2 + c])

    def own_grad(c):
        for way in range(2):
            back_copy(way, 1, c).wait_recv()
        for b in range(c * in_chunk, (c + 1) * in_chunk):
            value = grad_in[:, b * block : (b + 1) * block]
            value = value + back[0, 0, b].astype(F32) + back[1, 0, b].astype(F32)
            k = b - c * in_chunk
            gall[c, mine, k * block : (k + 1) * block] = value.astype(BF16)
        feat_start(gall, 1, c)

    def results(c, first):
        feat_arrive(gall, 1, c)
        term = lax.dot_general(
            fall[c, mine, :], gall[c], (((1,), (1,)), ((), ())), preferred_element_type=F32
        )
        wsum[:, :hid] = term if first else wsum[:, :hid] + term
        if sum_inside and c == finish[-1]:
            for k in range(1, n):
                piece_copy(k).start()
        grad_in[:, c * cw : (c + 1) * cw] = jnp.dot(w_rows, gall[c], preferred_element_type=F32)
        grad_in_copy(c).start()

    for k, c in enumerate(finish):
        own_grad(c)
        if k > 0:
            feat_pass(gall, 1, finish[k - 1])
        if k > 1:
            results(finish[k - 2], k == 2)
    feat_pass(gall, 1, finish[-1])
    if chunks > 1:
        results(finish[-2], chunks == 2)
    results(finish[-1], chunks == 1)

    if sum_inside:
        whole = wsum[pl.ds(pl.multiple_of(row * piece, piece), piece), :]
        for k in range(1, n):
            piece_copy(k).wait_recv()
            whole = whole + wland[k]
        wpiece[pl.ds(pl.multiple_of(row * piece, piece), piece), :] = whole * scale
        for k in range(1, n):
            total_copy(k).start()
    if sum_inside:
        for k in range(1, n):
            total_arrival(k).wait_recv()
    result = wpiece if sum_inside else wsum
    grad_w_out = pltpu.make_async_copy(result.at[:, pl.ds(0, hid)], grad_w_hbm, out_sem.at[1])
    grad_w_out.start()
    bias_cols = jnp.broadcast_to(result[:, hid : hid + 1], (width, width))
    grad_b[...] = jnp.sum(jnp.where(diagonal, bias_cols, 0.0), axis=0, keepdims=True)
    hidden_out.wait()
    grad_w_out.wait()
    for c in range(chunks):
        grad_in_copy(c).wait()

    for k, peer in enumerate((sib, opp, opp_sib)):
        weight_copy(k, peer).wait_send()
    for kind, buf in enumerate((fall, gall)):
        for c in range(chunks):
            feat_move(buf, kind, 0, c, fe, opp).wait_send()
            feat_move(buf, kind, 1, c, fe, sib).wait_send()
            feat_move(buf, kind, 2, c, opp, sib).wait_send()
    for way in range(2):
        for d in range(1, half + 1):
            for c in moves(way, d - 1):
                back_copy(way, d, c).wait_send()
    if sum_inside:
        for k in range(1, n):
            piece_copy(k).wait_send()
            total_copy(k).wait_send()


def local(feats, weight, bias, tile_cols, tile_values, cotangent):
    width, nodes = feats.shape
    hid = weight.shape[1]
    count, block = tile_values.shape[0], tile_values.shape[1]
    n = lax.axis_size("rows")
    row_blocks = nodes // block
    per_block = count // row_blocks
    chunks = 4 if n <= 8 else 2
    half = n // 2
    sum_inside = n == 8
    scale = 1.0 / math.sqrt(nodes * n)

    index = jnp.arange(count, dtype=jnp.int32)
    is_local = index % per_block < TL
    cols = jnp.where(is_local, tile_cols % row_blocks, tile_cols)
    key = tile_cols + jnp.where(is_local, n * row_blocks, 0)
    earlier = (key[None, :] < key[:, None]) | (
        (key[None, :] == key[:, None]) & (index[None, :] < index[:, None])
    )
    rank = jnp.sum(earlier.astype(jnp.int32), axis=1)
    placed = rank[None, :] == index[:, None]
    order = jnp.sum(jnp.where(placed, index[None, :], 0), axis=1)
    in_order = jnp.sum(jnp.where(placed, key[None, :], 0), axis=1)
    keep = jnp.concatenate([jnp.zeros((1,), F32), (in_order[1:] == in_order[:-1]).astype(F32)])
    dest = jnp.arange((n + 1) * row_blocks, dtype=jnp.int32)
    dest = jnp.where(dest < n * row_blocks, dest, dest + lax.axis_index("rows") * row_blocks)
    upto = jnp.sum((key[None, :] <= dest[:, None]).astype(jnp.int32), axis=1)
    below = jnp.sum((key[None, :] < dest[:, None]).astype(jnp.int32), axis=1)
    has = (upto > below).astype(F32)
    last = jnp.maximum(upto - 1, 0)

    smem = pl.BlockSpec(memory_space=pltpu.SMEM)
    vmem = pl.BlockSpec(memory_space=pltpu.VMEM)
    anywhere = pl.BlockSpec(memory_space=pl.ANY)
    dma = pltpu.SemaphoreType.DMA
    piece = width // n if sum_inside else 8
    hidden, grad_in, grad_w, grad_b = pl.pallas_call(
        functools.partial(kernel, n, chunks, sum_inside, scale),
        out_shape=(
            jax.ShapeDtypeStruct((width, nodes), BF16),
            jax.ShapeDtypeStruct((width, nodes), F32),
            jax.ShapeDtypeStruct((width, hid), F32),
            jax.ShapeDtypeStruct((1, width), F32),
        ),
        in_specs=[smem] * 5 + [vmem] + [anywhere] * 4,
        out_specs=(anywhere, anywhere, anywhere, vmem),
        scratch_shapes=[
            pltpu.VMEM((row_blocks, width, block), BF16),
            pltpu.VMEM((n * row_blocks, width, block), BF16),
            pltpu.VMEM((count, block, block), BF16),
            pltpu.VMEM((width, nodes), BF16),
            pltpu.VMEM((chunks, 4 * width, nodes // chunks), BF16),
            pltpu.VMEM((chunks, 4 * width, nodes // chunks), BF16),
            pltpu.VMEM((row_blocks, width, block), BF16),
            pltpu.VMEM((count, width, block), F32),
            pltpu.VMEM((count, width, block), F32),
            pltpu.VMEM((row_blocks, width, block), F32),
            pltpu.VMEM((width, nodes), BF16),
            pltpu.VMEM((width, nodes), F32),
            pltpu.VMEM((2, half, row_blocks, width, block), BF16),
            pltpu.VMEM((4 * width, hid), BF16),
            pltpu.VMEM((hid, 4 * width), BF16),
            pltpu.VMEM((width, block), F32),
            pltpu.VMEM((width, hid + block), F32),
            pltpu.VMEM((n if sum_inside else 1, piece, hid + block), F32),
            pltpu.VMEM((width, hid + block), F32),
            dma((3,)),
            dma((row_blocks,)),
            dma((2 + chunks,)),
            dma((3,)),
            dma((3,)),
            dma((2, half, chunks)),
            dma((2, half, chunks)),
            dma((2, 3, chunks)),
            dma((2, 3, chunks)),
            dma((2, half, chunks)),
            dma((2, half, chunks)),
            dma((n,)),
            dma((n,)),
            dma((n,)),
            dma((n,)),
        ],
        compiler_params=pltpu.CompilerParams(
            collective_id=0, has_side_effects=True, vmem_limit_bytes=52 * 1024 * 1024
        ),
        cost_estimate=pl.CostEstimate(
            flops=2 * 2 * count * width * block * block + 6 * width * hid * nodes,
            bytes_accessed=2 * count * block * block,
            transcendentals=width * nodes,
        ),
    )(
        cols,
        order,
            keep,
        last,
        has,
        bias[None, :],
        feats,
        weight,
        tile_values,
        cotangent,
    )
    bias_total = grad_b[0]
    if not sum_inside:
        grad_w, bias_total = lax.psum((grad_w * scale, bias_total * scale), "rows")
    return hidden, grad_in, grad_w, bias_total


def solution(mesh):
    placed = (
        P("feat", "rows"),
        P("feat", None),
        P("feat"),
        P("rows"),
        P("rows", None, None),
        P("feat", "rows"),
    )
    return jax.shard_map(
        local,
        mesh=mesh,
        in_specs=placed,
        out_specs=(P("feat", "rows"), P("feat", "rows"), P("feat", None), P("feat")),
        check_vma=False,
    )
```

```python
import functools
import math

import jax
import jax.numpy as jnp
from jax import lax
from jax.experimental import pallas as pl
from jax.experimental.pallas import tpu as pltpu
from jax.sharding import PartitionSpec as P

MESH = pl.DeviceIdType.MESH
TL = 4
F32 = jnp.float32
BF16 = jnp.bfloat16


def kernel(
    n,
    chunks,
    sum_inside,
    scale,
    cols,
    order,
    keep,
    last,
    has,
    bias,
    feats,
    weight,
    tiles_hbm,
    cot_hbm,
    hidden_hbm,
    grad_in_hbm,
    grad_w_hbm,
    grad_b,
    own,
    gbuf,
    tiles,
    cot,
    zall,
    gall,
    ubuf,
    tbuf,
    sbuf,
    zloc,
    hidden,
    grad_in,
    back,
    wall,
    wt,
    bias_acc,
    wsum,
    wland,
    wpiece,
    local_sem,
    feats_sem,
    out_sem,
    w_send,
    w_recv,
    ag_send,
    ag_recv,
    fe_send,
    fe_recv,
    rs_send,
    rs_recv,
    s1_send,
    s1_recv,
    s2_send,
    s2_recv,
):
    width, nodes = feats.shape
    block = tiles.shape[1]
    row_blocks = nodes // block
    per_block = tiles.shape[0] // row_blocks
    in_chunk = row_blocks // chunks
    cw = in_chunk * block
    half = n // 2
    ahead = 1 if chunks == 8 else 2
    row = lax.axis_index("rows")
    fe = lax.axis_index("feat")
    odd = lax.rem(row, 2)
    pos = (1 - odd) * (row // 2) + odd * (n - 1 - row // 2)

    def row_at(p):
        p = lax.rem(p + 2 * n, n)
        far = p // half
        return (1 - far) * (2 * p) + far * (2 * n - 1 - 2 * p)

    near = (row_at(pos + 1), row_at(pos - 1))
    sib = fe + 1 - 2 * lax.rem(fe, 2)
    opp = lax.rem(fe + 2, 4)
    opp_sib = lax.rem(sib + 2, 4)

    tile_copy = pltpu.make_async_copy(tiles_hbm, tiles, local_sem.at[0])
    cot_copy = pltpu.make_async_copy(cot_hbm, cot, local_sem.at[1])
    feats_copies = [
        pltpu.make_async_copy(
            feats.at[:, pl.ds(b * block, block)],
            own.at[b],
            feats_sem.at[b],
        )
        for b in range(row_blocks)
    ]
    for copy in feats_copies:
        copy.start()
    mine = pl.ds(pl.multiple_of(fe * width, width), width)
    weight_in = pltpu.make_async_copy(weight, wall.at[mine, :], local_sem.at[2])
    weight_in.start()

    barrier = pltpu.get_barrier_semaphore()
    if sum_inside:
        others = [lax.rem(row + k, n) for k in range(1, n)]
    else:
        others = list(near)
    for peer in others:
        pl.semaphore_signal(barrier, inc=1, device_id={"rows": peer}, device_id_type=MESH)
    for peer in (sib, opp, opp_sib):
        pl.semaphore_signal(barrier, inc=1, device_id={"feat": peer}, device_id_type=MESH)

    for copy in feats_copies:
        copy.wait()
    tile_copy.start()
    cot_copy.start()
    weight_in.wait()
    pl.semaphore_wait(barrier, len(others) + 3)

    def span(owner, c):
        return gbuf.at[pl.ds(owner * row_blocks + c * in_chunk, in_chunk)]

    def gather_copy(way, d, c):
        sign = 1 - 2 * way
        at = span(row_at(pos - sign * d), c)
        src = own.at[pl.ds(c * in_chunk, in_chunk)] if d == 0 else at
        return pltpu.make_async_remote_copy(
            src_ref=src,
            dst_ref=at,
            send_sem=ag_send.at[way, d, c],
            recv_sem=ag_recv.at[way, d, c],
            device_id={"rows": near[way]},
            device_id_type=MESH,
        )

    def gather_arrival(way, d, c):
        sign = 1 - 2 * way
        at = span(row_at(pos - sign * (d + 1)), c)
        return pltpu.make_async_remote_copy(
            src_ref=at,
            dst_ref=at,
            send_sem=ag_send.at[way, d, c],
            recv_sem=ag_recv.at[way, d, c],
            device_id={"rows": near[way]},
            device_id_type=MESH,
        )

    def moves(way, d):
        if d < half - 1:
            return list(range(chunks))
        if way == 0:
            return list(range(chunks // 2))
        return list(range(chunks // 2, chunks))

    def weight_copy(k, peer):
        at = wall.at[pl.ds(pl.multiple_of(fe * width, width), width), :]
        return pltpu.make_async_remote_copy(
            src_ref=at,
            dst_ref=at,
            send_sem=w_send.at[k],
            recv_sem=w_recv.at[k],
            device_id={"feat": peer},
            device_id_type=MESH,
        )

    def weight_arrival(k, peer):
        at = wall.at[pl.ds(pl.multiple_of(peer * width, width), width), :]
        return pltpu.make_async_remote_copy(
            src_ref=at,
            dst_ref=at,
            send_sem=w_send.at[k],
            recv_sem=w_recv.at[k],
            device_id={"feat": peer},
            device_id_type=MESH,
        )

    for c in range(chunks):
        for way in range(2):
            if c in moves(way, 0):
                gather_copy(way, 0, c).start()
    for k, peer in enumerate((sib, opp, opp_sib)):
        weight_copy(k, peer).start()
    def products(get, r, first, count):
        left = jnp.concatenate([get(r * per_block + first + t) for t in range(count)], axis=1)
        right = jnp.concatenate([tiles[r * per_block + first + t] for t in range(count)], axis=1)
        return lax.dot_general(left, right, (((1,), (1,)), ((), ())), preferred_element_type=F32)

    def local_products(r):
        zloc[r] = products(lambda i: own[cols[i]], r, 0, TL)

    for b in range(row_blocks):
        gbuf[row * row_blocks + b] = own[b]
    done = 0
    for d in range(1, half):
        for c in range(chunks):
            for way in range(2):
                if c in moves(way, d - 1):
                    gather_arrival(way, d - 1, c).wait_recv()
                if c in moves(way, d):
                    gather_copy(way, d, c).start()
            if d == 1 and c == 0:
                tile_copy.wait()
            if done < row_blocks:
                for r in range(done, min(done + ahead, row_blocks)):
                    local_products(r)
                done = min(done + ahead, row_blocks)
        if d == 1:
            for k, peer in enumerate((sib, opp, opp_sib)):
                weight_arrival(k, peer).wait_recv()
            wt[...] = wall[...].astype(F32).T.astype(BF16)
            cot_copy.wait()
    for r in range(done, row_blocks):
        local_products(r)
    for way in range(2):
        for c in moves(way, half - 1):
            gather_arrival(way, half - 1, c).wait_recv()

    def feat_move(buf, kind, hop, c, owner, peer):
        at = buf.at[c, pl.ds(pl.multiple_of(owner * width, width), width), :]
        return pltpu.make_async_remote_copy(
            src_ref=at,
            dst_ref=at,
            send_sem=fe_send.at[kind, hop, c],
            recv_sem=fe_recv.at[kind, hop, c],
            device_id={"feat": peer},
            device_id_type=MESH,
        )

    def feat_start(buf, kind, c):
        feat_move(buf, kind, 0, c, fe, opp).start()
        feat_move(buf, kind, 1, c, fe, sib).start()

    def feat_pass(buf, kind, c):
        feat_move(buf, kind, 0, c, opp, opp).wait_recv()
        feat_move(buf, kind, 2, c, opp, sib).start()

    def feat_arrive(buf, kind, c):
        feat_move(buf, kind, 1, c, sib, sib).wait_recv()
        feat_move(buf, kind, 2, c, opp_sib, sib).wait_recv()

    for c in range(chunks):

        def one_row(r, carry, c=c):
            at = c * in_chunk + r
            total = zloc[at] + products(lambda i: gbuf[cols[i]], at, TL, per_block - TL)
            zall[c, mine, pl.ds(pl.multiple_of(r * block, block), block)] = total.astype(BF16)
            return carry

        lax.fori_loop(0, in_chunk, one_row, 0)
        feat_start(zall, 0, c)
        if c > 0:
            feat_pass(zall, 0, c - 1)
    feat_pass(zall, 0, chunks - 1)

    w_cols = wt[mine, :]
    w_rows = wall[mine, :]
    diagonal = lax.broadcasted_iota(jnp.int32, (width, width), 0) == lax.broadcasted_iota(
        jnp.int32, (width, width), 1
    )
    bias_row = jnp.broadcast_to(bias[...], (width, width))
    bias_col = jnp.sum(jnp.where(diagonal, bias_row, 0.0), axis=1, keepdims=True)
    for c in range(chunks):
        feat_arrive(zall, 0, c)
        pre = jnp.dot(w_cols, zall[c], preferred_element_type=F32) + bias_col
        sigma = jax.nn.sigmoid(pre)
        hidden[:, c * cw : (c + 1) * cw] = (pre * sigma).astype(BF16)
        g = cot[:, c * cw : (c + 1) * cw].astype(F32) * (sigma * (1.0 + pre * (1.0 - sigma)))
        gall[c, mine, :] = g.astype(BF16)
        feat_start(gall, 1, c)
        folded = g[:, :block]
        for b in range(1, in_chunk):
            folded = folded + g[:, b * block : (b + 1) * block]
        bias_acc[...] = folded if c == 0 else bias_acc[...] + folded
        if c > 0:
            feat_pass(gall, 1, c - 1)
    feat_pass(gall, 1, chunks - 1)
    hidden_out = pltpu.make_async_copy(hidden, hidden_hbm, out_sem.at[0])
    hidden_out.start()

    def terms(r, first, count):
        right = jnp.concatenate([tiles[r * per_block + first + t] for t in range(count)], axis=1)
        out = jnp.dot(ubuf[r], right, preferred_element_type=F32)
        for t in range(count):
            tbuf[r * per_block + first + t] = out[:, t * block : (t + 1) * block]

    w_sum = jnp.zeros((width, wall.shape[1]), F32)
    for c in range(chunks):
        feat_arrive(gall, 1, c)
        u = jnp.dot(w_rows, gall[c], preferred_element_type=F32).astype(BF16)
        for b in range(in_chunk):
            ubuf[c * in_chunk + b] = u[:, b * block : (b + 1) * block]
            terms(c * in_chunk + b, TL, per_block - TL)
        w_sum += lax.dot_general(
            zall[c, mine, :], gall[c], (((1,), (1,)), ((), ())), preferred_element_type=F32
        )
    hid = wall.shape[1]
    wsum[:, :hid] = w_sum
    wsum[:, hid:] = jnp.broadcast_to(jnp.sum(bias_acc[...], axis=1, keepdims=True), bias_acc.shape)

    piece = width // n if sum_inside else width

    def piece_at(ref, owner):
        return ref.at[pl.ds(pl.multiple_of(owner * piece, piece), piece), :]

    def piece_copy(k):
        to = lax.rem(row + k, n)
        return pltpu.make_async_remote_copy(
            src_ref=piece_at(wsum, to),
            dst_ref=wland.at[k],
            send_sem=s1_send.at[k],
            recv_sem=s1_recv.at[k],
            device_id={"rows": to},
            device_id_type=MESH,
        )

    def total_copy(k):
        to = lax.rem(row + k, n)
        return pltpu.make_async_remote_copy(
            src_ref=piece_at(wpiece, row),
            dst_ref=piece_at(wpiece, row),
            send_sem=s2_send.at[k],
            recv_sem=s2_recv.at[k],
            device_id={"rows": to},
            device_id_type=MESH,
        )

    def total_arrival(k):
        owner = lax.rem(row + n - k, n)
        return pltpu.make_async_remote_copy(
            src_ref=piece_at(wpiece, owner),
            dst_ref=piece_at(wpiece, owner),
            send_sem=s2_send.at[k],
            recv_sem=s2_recv.at[k],
            device_id={"rows": owner},
            device_id_type=MESH,
        )

    if sum_inside:
        for k in range(1, n):
            piece_copy(k).start()

    group = 8
    locals_count = row_blocks * TL
    remote_count = tiles.shape[0] - locals_count

    def running_sums(first, count):
        def some_sums(i, running):
            for j in range(group):
                at = first + i * group + j
                running = tbuf[order[at]] + keep[at] * running
                sbuf[at] = running
            return running

        lax.fori_loop(0, count // group, some_sums, jnp.zeros((width, block), F32))

    running_sums(0, remote_count)

    for way in range(2):
        for d in range(half):
            for c in moves(way, d):
                gather_copy(way, d, c).wait_send()

    def own_term(at):
        return sbuf[last[at]] * has[at]

    def back_copy(way, d, c):
        sign = 1 - 2 * way
        return pltpu.make_async_remote_copy(
            src_ref=span(row_at(pos + sign * d), c),
            dst_ref=back.at[way, d - 1, pl.ds(c * in_chunk, in_chunk)],
            send_sem=rs_send.at[way, d - 1, c],
            recv_sem=rs_recv.at[way, d - 1, c],
            device_id={"rows": near[way]},
            device_id_type=MESH,
        )

    def send_back(way, d, c):
        joined = d < half and c in moves(way, d)
        if joined:
            back_copy(way, d + 1, c).wait_recv()
        sign = 1 - 2 * way
        owner = row_at(pos + sign * d)
        for b in range(c * in_chunk, (c + 1) * in_chunk):
            at = owner * row_blocks + b
            value = own_term(at)
            if joined:
                value = value + back[way, d, b].astype(F32)
            gbuf[at] = value.astype(BF16)
        back_copy(way, d, c).start()

    orders = (
        list(range(chunks // 2, chunks)) + list(range(chunks // 2)),
        list(range(chunks)),
    )
    done = 0
    for d in range(half, 0, -1):
        for k in range(chunks):
            for way in range(2):
                if orders[way][k] in moves(way, d - 1):
                    send_back(way, d, orders[way][k])
            if d < half or half == 1:
                for r in range(done, min(done + ahead, row_blocks)):
                    terms(r, 0, TL)
                done = min(done + ahead, row_blocks)
        if sum_inside and d == half - 1:
            whole = wsum[pl.ds(pl.multiple_of(row * piece, piece), piece), :]
            for k in range(1, n):
                piece_copy(k).wait_recv()
                whole = whole + wland[k]
            wpiece[pl.ds(pl.multiple_of(row * piece, piece), piece), :] = whole * scale
            for k in range(1, n):
                total_copy(k).start()
    for r in range(done, row_blocks):
        terms(r, 0, TL)
    running_sums(remote_count, locals_count)
    for b in range(row_blocks):
        at = n * row_blocks + b
        grad_in[:, b * block : (b + 1) * block] = own_term(row * row_blocks + b) + own_term(at)

    def grad_in_copy(c):
        at = pl.ds(c * cw, cw)
        return pltpu.make_async_copy(grad_in.at[:, at], grad_in_hbm.at[:, at], out_sem.at[2 + c])

    for c in range(chunks):
        for way in range(2):
            back_copy(way, 1, c).wait_recv()
        for b in range(c * in_chunk, (c + 1) * in_chunk):
            value = grad_in[:, b * block : (b + 1) * block]
            value = value + back[0, 0, b].astype(F32) + back[1, 0, b].astype(F32)
            grad_in[:, b * block : (b + 1) * block] = value
        grad_in_copy(c).start()

    if sum_inside:
        for k in range(1, n):
            total_arrival(k).wait_recv()
    result = wpiece if sum_inside else wsum
    grad_w_out = pltpu.make_async_copy(result.at[:, pl.ds(0, hid)], grad_w_hbm, out_sem.at[1])
    grad_w_out.start()
    bias_cols = jnp.broadcast_to(result[:, hid : hid + 1], (width, width))
    grad_b[...] = jnp.sum(jnp.where(diagonal, bias_cols, 0.0), axis=0, keepdims=True)
    hidden_out.wait()
    grad_w_out.wait()
    for c in range(chunks):
        grad_in_copy(c).wait()

    for k, peer in enumerate((sib, opp, opp_sib)):
        weight_copy(k, peer).wait_send()
    for kind, buf in enumerate((zall, gall)):
        for c in range(chunks):
            feat_move(buf, kind, 0, c, fe, opp).wait_send()
            feat_move(buf, kind, 1, c, fe, sib).wait_send()
            feat_move(buf, kind, 2, c, opp, sib).wait_send()
    for way in range(2):
        for d in range(1, half + 1):
            for c in moves(way, d - 1):
                back_copy(way, d, c).wait_send()
    if sum_inside:
        for k in range(1, n):
            piece_copy(k).wait_send()
            total_copy(k).wait_send()


def local(feats, weight, bias, tile_cols, tile_values, cotangent):
    width, nodes = feats.shape
    hid = weight.shape[1]
    count, block = tile_values.shape[0], tile_values.shape[1]
    n = lax.axis_size("rows")
    row_blocks = nodes // block
    per_block = count // row_blocks
    chunks = 8 if n <= 8 else 2
    half = n // 2
    sum_inside = n == 8
    scale = 1.0 / math.sqrt(nodes * n)

    index = jnp.arange(count, dtype=jnp.int32)
    is_local = index % per_block < TL
    cols = jnp.where(is_local, tile_cols % row_blocks, tile_cols)
    key = tile_cols + jnp.where(is_local, n * row_blocks, 0)
    earlier = (key[None, :] < key[:, None]) | (
        (key[None, :] == key[:, None]) & (index[None, :] < index[:, None])
    )
    rank = jnp.sum(earlier.astype(jnp.int32), axis=1)
    placed = rank[None, :] == index[:, None]
    order = jnp.sum(jnp.where(placed, index[None, :], 0), axis=1)
    in_order = jnp.sum(jnp.where(placed, key[None, :], 0), axis=1)
    keep = jnp.concatenate([jnp.zeros((1,), F32), (in_order[1:] == in_order[:-1]).astype(F32)])
    dest = jnp.arange((n + 1) * row_blocks, dtype=jnp.int32)
    dest = jnp.where(dest < n * row_blocks, dest, dest + lax.axis_index("rows") * row_blocks)
    upto = jnp.sum((key[None, :] <= dest[:, None]).astype(jnp.int32), axis=1)
    below = jnp.sum((key[None, :] < dest[:, None]).astype(jnp.int32), axis=1)
    has = (upto > below).astype(F32)
    last = jnp.maximum(upto - 1, 0)

    smem = pl.BlockSpec(memory_space=pltpu.SMEM)
    vmem = pl.BlockSpec(memory_space=pltpu.VMEM)
    anywhere = pl.BlockSpec(memory_space=pl.ANY)
    dma = pltpu.SemaphoreType.DMA
    piece = width // n if sum_inside else 8
    hidden, grad_in, grad_w, grad_b = pl.pallas_call(
        functools.partial(kernel, n, chunks, sum_inside, scale),
        out_shape=(
            jax.ShapeDtypeStruct((width, nodes), BF16),
            jax.ShapeDtypeStruct((width, nodes), F32),
            jax.ShapeDtypeStruct((width, hid), F32),
            jax.ShapeDtypeStruct((1, width), F32),
        ),
        in_specs=[smem] * 5 + [vmem] + [anywhere] * 4,
        out_specs=(anywhere, anywhere, anywhere, vmem),
        scratch_shapes=[
            pltpu.VMEM((row_blocks, width, block), BF16),
            pltpu.VMEM((n * row_blocks, width, block), BF16),
            pltpu.VMEM((count, block, block), BF16),
            pltpu.VMEM((width, nodes), BF16),
            pltpu.VMEM((chunks, 4 * width, nodes // chunks), BF16),
            pltpu.VMEM((chunks, 4 * width, nodes // chunks), BF16),
            pltpu.VMEM((row_blocks, width, block), BF16),
            pltpu.VMEM((count, width, block), F32),
            pltpu.VMEM((count, width, block), F32),
            pltpu.VMEM((row_blocks, width, block), F32),
            pltpu.VMEM((width, nodes), BF16),
            pltpu.VMEM((width, nodes), F32),
            pltpu.VMEM((2, half, row_blocks, width, block), BF16),
            pltpu.VMEM((4 * width, hid), BF16),
            pltpu.VMEM((hid, 4 * width), BF16),
            pltpu.VMEM((width, block), F32),
            pltpu.VMEM((width, hid + block), F32),
            pltpu.VMEM((n if sum_inside else 1, piece, hid + block), F32),
            pltpu.VMEM((width, hid + block), F32),
            dma((3,)),
            dma((row_blocks,)),
            dma((2 + chunks,)),
            dma((3,)),
            dma((3,)),
            dma((2, half, chunks)),
            dma((2, half, chunks)),
            dma((2, 3, chunks)),
            dma((2, 3, chunks)),
            dma((2, half, chunks)),
            dma((2, half, chunks)),
            dma((n,)),
            dma((n,)),
            dma((n,)),
            dma((n,)),
        ],
        compiler_params=pltpu.CompilerParams(
            collective_id=0, has_side_effects=True, vmem_limit_bytes=52 * 1024 * 1024
        ),
        cost_estimate=pl.CostEstimate(
            flops=2 * 2 * count * width * block * block + 6 * width * hid * nodes,
            bytes_accessed=2 * count * block * block,
            transcendentals=width * nodes,
        ),
    )(
        cols,
        order,
            keep,
        last,
        has,
        bias[None, :],
        feats,
        weight,
        tile_values,
        cotangent,
    )
    bias_total = grad_b[0]
    if not sum_inside:
        grad_w, bias_total = lax.psum((grad_w * scale, bias_total * scale), "rows")
    return hidden, grad_in, grad_w, bias_total


def solution(mesh):
    placed = (
        P("feat", "rows"),
        P("feat", None),
        P("feat"),
        P("rows"),
        P("rows", None, None),
        P("feat", "rows"),
    )
    return jax.shard_map(
        local,
        mesh=mesh,
        in_specs=placed,
        out_specs=(P("feat", "rows"), P("feat", "rows"), P("feat", None), P("feat")),
        check_vma=False,
    )
```

```python
import functools
import math

import jax
import jax.numpy as jnp
from jax import lax
from jax.experimental import pallas as pl
from jax.experimental.pallas import tpu as pltpu
from jax.sharding import PartitionSpec as P

MESH = pl.DeviceIdType.MESH
TL = 4
F32 = jnp.float32
BF16 = jnp.bfloat16


def kernel(
    n,
    chunks,
    sum_inside,
    scale,
    cols,
    order,
    keep,
    last,
    has,
    bias,
    feats,
    weight,
    tiles_hbm,
    cot_hbm,
    hidden_hbm,
    grad_in_hbm,
    grad_w_hbm,
    grad_b,
    own,
    gbuf,
    tiles,
    cot,
    zall,
    gall,
    ubuf,
    tbuf,
    sbuf,
    zloc,
    hidden,
    grad_in,
    back,
    wall,
    wt,
    bias_acc,
    wsum,
    wland,
    wpiece,
    local_sem,
    feats_sem,
    out_sem,
    w_send,
    w_recv,
    ag_send,
    ag_recv,
    fe_send,
    fe_recv,
    rs_send,
    rs_recv,
    s1_send,
    s1_recv,
    s2_send,
    s2_recv,
):
    width, nodes = feats.shape
    block = tiles.shape[1]
    row_blocks = nodes // block
    per_block = tiles.shape[0] // row_blocks
    in_chunk = row_blocks // chunks
    cw = in_chunk * block
    half = n // 2
    row = lax.axis_index("rows")
    fe = lax.axis_index("feat")
    odd = lax.rem(row, 2)
    pos = (1 - odd) * (row // 2) + odd * (n - 1 - row // 2)

    def row_at(p):
        p = lax.rem(p + 2 * n, n)
        far = p // half
        return (1 - far) * (2 * p) + far * (2 * n - 1 - 2 * p)

    near = (row_at(pos + 1), row_at(pos - 1))
    sib = fe + 1 - 2 * lax.rem(fe, 2)
    opp = lax.rem(fe + 2, 4)
    opp_sib = lax.rem(sib + 2, 4)

    tile_copy = pltpu.make_async_copy(tiles_hbm, tiles, local_sem.at[0])
    cot_copy = pltpu.make_async_copy(cot_hbm, cot, local_sem.at[1])
    feats_copies = [
        pltpu.make_async_copy(
            feats.at[:, pl.ds(b * block, block)],
            own.at[b],
            feats_sem.at[b],
        )
        for b in range(row_blocks)
    ]
    for copy in feats_copies:
        copy.start()
    mine = pl.ds(pl.multiple_of(fe * width, width), width)
    weight_in = pltpu.make_async_copy(weight, wall.at[mine, :], local_sem.at[2])
    weight_in.start()

    barrier = pltpu.get_barrier_semaphore()
    if sum_inside:
        others = [lax.rem(row + k, n) for k in range(1, n)]
    else:
        others = list(near)
    for peer in others:
        pl.semaphore_signal(barrier, inc=1, device_id={"rows": peer}, device_id_type=MESH)
    for peer in (sib, opp, opp_sib):
        pl.semaphore_signal(barrier, inc=1, device_id={"feat": peer}, device_id_type=MESH)

    for copy in feats_copies:
        copy.wait()
    tile_copy.start()
    cot_copy.start()
    weight_in.wait()
    pl.semaphore_wait(barrier, len(others) + 3)

    def span(owner, c):
        return gbuf.at[pl.ds(owner * row_blocks + c * in_chunk, in_chunk)]

    def gather_copy(way, d, c):
        sign = 1 - 2 * way
        at = span(row_at(pos - sign * d), c)
        src = own.at[pl.ds(c * in_chunk, in_chunk)] if d == 0 else at
        return pltpu.make_async_remote_copy(
            src_ref=src,
            dst_ref=at,
            send_sem=ag_send.at[way, d, c],
            recv_sem=ag_recv.at[way, d, c],
            device_id={"rows": near[way]},
            device_id_type=MESH,
        )

    def gather_arrival(way, d, c):
        sign = 1 - 2 * way
        at = span(row_at(pos - sign * (d + 1)), c)
        return pltpu.make_async_remote_copy(
            src_ref=at,
            dst_ref=at,
            send_sem=ag_send.at[way, d, c],
            recv_sem=ag_recv.at[way, d, c],
            device_id={"rows": near[way]},
            device_id_type=MESH,
        )

    def moves(way, d):
        if d < half - 1:
            return list(range(chunks))
        if way == 0:
            return list(range(chunks // 2))
        return list(range(chunks // 2, chunks))

    def weight_copy(k, peer):
        at = wall.at[pl.ds(pl.multiple_of(fe * width, width), width), :]
        return pltpu.make_async_remote_copy(
            src_ref=at,
            dst_ref=at,
            send_sem=w_send.at[k],
            recv_sem=w_recv.at[k],
            device_id={"feat": peer},
            device_id_type=MESH,
        )

    def weight_arrival(k, peer):
        at = wall.at[pl.ds(pl.multiple_of(peer * width, width), width), :]
        return pltpu.make_async_remote_copy(
            src_ref=at,
            dst_ref=at,
            send_sem=w_send.at[k],
            recv_sem=w_recv.at[k],
            device_id={"feat": peer},
            device_id_type=MESH,
        )

    for c in range(chunks):
        for way in range(2):
            if c in moves(way, 0):
                gather_copy(way, 0, c).start()
    for k, peer in enumerate((sib, opp, opp_sib)):
        weight_copy(k, peer).start()
    def products(get, r, first, count):
        left = jnp.concatenate([get(r * per_block + first + t) for t in range(count)], axis=1)
        right = jnp.concatenate([tiles[r * per_block + first + t] for t in range(count)], axis=1)
        return lax.dot_general(left, right, (((1,), (1,)), ((), ())), preferred_element_type=F32)

    def local_products(r):
        zloc[r] = products(lambda i: own[cols[i]], r, 0, TL)

    for b in range(row_blocks):
        gbuf[row * row_blocks + b] = own[b]
    done = 0
    for d in range(1, half):
        for c in range(chunks):
            for way in range(2):
                if c in moves(way, d - 1):
                    gather_arrival(way, d - 1, c).wait_recv()
                if c in moves(way, d):
                    gather_copy(way, d, c).start()
            if d == 1 and c == 0:
                tile_copy.wait()
            if done < row_blocks:
                for r in range(done, min(done + 4, row_blocks)):
                    local_products(r)
                done = min(done + 4, row_blocks)
        if d == 1:
            for k, peer in enumerate((sib, opp, opp_sib)):
                weight_arrival(k, peer).wait_recv()
            wt[...] = wall[...].astype(F32).T.astype(BF16)
            cot_copy.wait()
    for r in range(done, row_blocks):
        local_products(r)
    for way in range(2):
        for c in moves(way, half - 1):
            gather_arrival(way, half - 1, c).wait_recv()

    def feat_move(buf, kind, hop, c, owner, peer):
        at = buf.at[c, pl.ds(pl.multiple_of(owner * width, width), width), :]
        return pltpu.make_async_remote_copy(
            src_ref=at,
            dst_ref=at,
            send_sem=fe_send.at[kind, hop, c],
            recv_sem=fe_recv.at[kind, hop, c],
            device_id={"feat": peer},
            device_id_type=MESH,
        )

    def feat_start(buf, kind, c):
        feat_move(buf, kind, 0, c, fe, opp).start()
        feat_move(buf, kind, 1, c, fe, sib).start()

    def feat_pass(buf, kind, c):
        feat_move(buf, kind, 0, c, opp, opp).wait_recv()
        feat_move(buf, kind, 2, c, opp, sib).start()

    def feat_arrive(buf, kind, c):
        feat_move(buf, kind, 1, c, sib, sib).wait_recv()
        feat_move(buf, kind, 2, c, opp_sib, sib).wait_recv()

    for c in range(chunks):

        def one_row(r, carry, c=c):
            at = c * in_chunk + r
            total = zloc[at] + products(lambda i: gbuf[cols[i]], at, TL, per_block - TL)
            zall[c, mine, pl.ds(pl.multiple_of(r * block, block), block)] = total.astype(BF16)
            return carry

        lax.fori_loop(0, in_chunk, one_row, 0)
        feat_start(zall, 0, c)
        if c > 0:
            feat_pass(zall, 0, c - 1)
    feat_pass(zall, 0, chunks - 1)

    w_cols = wt[mine, :]
    w_rows = wall[mine, :]
    diagonal = lax.broadcasted_iota(jnp.int32, (width, width), 0) == lax.broadcasted_iota(
        jnp.int32, (width, width), 1
    )
    bias_row = jnp.broadcast_to(bias[...], (width, width))
    bias_col = jnp.sum(jnp.where(diagonal, bias_row, 0.0), axis=1, keepdims=True)
    for c in range(chunks):
        feat_arrive(zall, 0, c)
        pre = jnp.dot(w_cols, zall[c], preferred_element_type=F32) + bias_col
        sigma = jax.nn.sigmoid(pre)
        hidden[:, c * cw : (c + 1) * cw] = (pre * sigma).astype(BF16)
        g = cot[:, c * cw : (c + 1) * cw].astype(F32) * (sigma * (1.0 + pre * (1.0 - sigma)))
        gall[c, mine, :] = g.astype(BF16)
        feat_start(gall, 1, c)
        folded = g[:, :block]
        for b in range(1, in_chunk):
            folded = folded + g[:, b * block : (b + 1) * block]
        bias_acc[...] = folded if c == 0 else bias_acc[...] + folded
        if c > 0:
            feat_pass(gall, 1, c - 1)
    feat_pass(gall, 1, chunks - 1)
    hidden_out = pltpu.make_async_copy(hidden, hidden_hbm, out_sem.at[0])
    hidden_out.start()

    def terms(r, first, count):
        right = jnp.concatenate([tiles[r * per_block + first + t] for t in range(count)], axis=1)
        out = jnp.dot(ubuf[r], right, preferred_element_type=F32)
        for t in range(count):
            tbuf[r * per_block + first + t] = out[:, t * block : (t + 1) * block]

    w_sum = jnp.zeros((width, wall.shape[1]), F32)
    for c in range(chunks):
        feat_arrive(gall, 1, c)
        u = jnp.dot(w_rows, gall[c], preferred_element_type=F32).astype(BF16)
        for b in range(in_chunk):
            ubuf[c * in_chunk + b] = u[:, b * block : (b + 1) * block]
            terms(c * in_chunk + b, TL, per_block - TL)
        w_sum += lax.dot_general(
            zall[c, mine, :], gall[c], (((1,), (1,)), ((), ())), preferred_element_type=F32
        )
    hid = wall.shape[1]
    wsum[:, :hid] = w_sum
    wsum[:, hid:] = jnp.broadcast_to(jnp.sum(bias_acc[...], axis=1, keepdims=True), bias_acc.shape)

    piece = width // n if sum_inside else width

    def piece_at(ref, owner):
        return ref.at[pl.ds(pl.multiple_of(owner * piece, piece), piece), :]

    def piece_copy(k):
        to = lax.rem(row + k, n)
        return pltpu.make_async_remote_copy(
            src_ref=piece_at(wsum, to),
            dst_ref=wland.at[k],
            send_sem=s1_send.at[k],
            recv_sem=s1_recv.at[k],
            device_id={"rows": to},
            device_id_type=MESH,
        )

    def total_copy(k):
        to = lax.rem(row + k, n)
        return pltpu.make_async_remote_copy(
            src_ref=piece_at(wpiece, row),
            dst_ref=piece_at(wpiece, row),
            send_sem=s2_send.at[k],
            recv_sem=s2_recv.at[k],
            device_id={"rows": to},
            device_id_type=MESH,
        )

    def total_arrival(k):
        owner = lax.rem(row + n - k, n)
        return pltpu.make_async_remote_copy(
            src_ref=piece_at(wpiece, owner),
            dst_ref=piece_at(wpiece, owner),
            send_sem=s2_send.at[k],
            recv_sem=s2_recv.at[k],
            device_id={"rows": owner},
            device_id_type=MESH,
        )

    if sum_inside:
        for k in range(1, n):
            piece_copy(k).start()

    group = 8
    locals_count = row_blocks * TL
    remote_count = tiles.shape[0] - locals_count

    def running_sums(first, count):
        def some_sums(i, running):
            for j in range(group):
                at = first + i * group + j
                running = tbuf[order[at]] + keep[at] * running
                sbuf[at] = running
            return running

        lax.fori_loop(0, count // group, some_sums, jnp.zeros((width, block), F32))

    running_sums(0, remote_count)

    for way in range(2):
        for d in range(half):
            for c in moves(way, d):
                gather_copy(way, d, c).wait_send()

    def own_term(at):
        return sbuf[last[at]] * has[at]

    def back_copy(way, d, c):
        sign = 1 - 2 * way
        return pltpu.make_async_remote_copy(
            src_ref=span(row_at(pos + sign * d), c),
            dst_ref=back.at[way, d - 1, pl.ds(c * in_chunk, in_chunk)],
            send_sem=rs_send.at[way, d - 1, c],
            recv_sem=rs_recv.at[way, d - 1, c],
            device_id={"rows": near[way]},
            device_id_type=MESH,
        )

    def send_back(way, d, c):
        joined = d < half and c in moves(way, d)
        if joined:
            back_copy(way, d + 1, c).wait_recv()
        sign = 1 - 2 * way
        owner = row_at(pos + sign * d)
        for b in range(c * in_chunk, (c + 1) * in_chunk):
            at = owner * row_blocks + b
            value = own_term(at)
            if joined:
                value = value + back[way, d, b].astype(F32)
            gbuf[at] = value.astype(BF16)
        back_copy(way, d, c).start()

    orders = (
        list(range(chunks // 2, chunks)) + list(range(chunks // 2)),
        list(range(chunks)),
    )
    done = 0
    for d in range(half, 0, -1):
        for k in range(chunks):
            for way in range(2):
                if orders[way][k] in moves(way, d - 1):
                    send_back(way, d, orders[way][k])
            if d < half or half == 1:
                for r in range(done, min(done + 4, row_blocks)):
                    terms(r, 0, TL)
                done = min(done + 4, row_blocks)
        if sum_inside and d == half - 1:
            whole = wsum[pl.ds(pl.multiple_of(row * piece, piece), piece), :]
            for k in range(1, n):
                piece_copy(k).wait_recv()
                whole = whole + wland[k]
            wpiece[pl.ds(pl.multiple_of(row * piece, piece), piece), :] = whole * scale
            for k in range(1, n):
                total_copy(k).start()
    for r in range(done, row_blocks):
        terms(r, 0, TL)
    running_sums(remote_count, locals_count)
    for b in range(row_blocks):
        at = n * row_blocks + b
        grad_in[:, b * block : (b + 1) * block] = own_term(row * row_blocks + b) + own_term(at)

    def grad_in_copy(c):
        at = pl.ds(c * cw, cw)
        return pltpu.make_async_copy(grad_in.at[:, at], grad_in_hbm.at[:, at], out_sem.at[2 + c])

    for c in range(chunks):
        for way in range(2):
            back_copy(way, 1, c).wait_recv()
        for b in range(c * in_chunk, (c + 1) * in_chunk):
            value = grad_in[:, b * block : (b + 1) * block]
            value = value + back[0, 0, b].astype(F32) + back[1, 0, b].astype(F32)
            grad_in[:, b * block : (b + 1) * block] = value
        grad_in_copy(c).start()

    if sum_inside:
        for k in range(1, n):
            total_arrival(k).wait_recv()
    result = wpiece if sum_inside else wsum
    grad_w_out = pltpu.make_async_copy(result.at[:, pl.ds(0, hid)], grad_w_hbm, out_sem.at[1])
    grad_w_out.start()
    bias_cols = jnp.broadcast_to(result[:, hid : hid + 1], (width, width))
    grad_b[...] = jnp.sum(jnp.where(diagonal, bias_cols, 0.0), axis=0, keepdims=True)
    hidden_out.wait()
    grad_w_out.wait()
    for c in range(chunks):
        grad_in_copy(c).wait()

    for k, peer in enumerate((sib, opp, opp_sib)):
        weight_copy(k, peer).wait_send()
    for kind, buf in enumerate((zall, gall)):
        for c in range(chunks):
            feat_move(buf, kind, 0, c, fe, opp).wait_send()
            feat_move(buf, kind, 1, c, fe, sib).wait_send()
            feat_move(buf, kind, 2, c, opp, sib).wait_send()
    for way in range(2):
        for d in range(1, half + 1):
            for c in moves(way, d - 1):
                back_copy(way, d, c).wait_send()
    if sum_inside:
        for k in range(1, n):
            piece_copy(k).wait_send()
            total_copy(k).wait_send()


def local(feats, weight, bias, tile_cols, tile_values, cotangent):
    width, nodes = feats.shape
    hid = weight.shape[1]
    count, block = tile_values.shape[0], tile_values.shape[1]
    n = lax.axis_size("rows")
    row_blocks = nodes // block
    per_block = count // row_blocks
    chunks = 2
    half = n // 2
    sum_inside = n == 8
    scale = 1.0 / math.sqrt(nodes * n)

    index = jnp.arange(count, dtype=jnp.int32)
    is_local = index % per_block < TL
    cols = jnp.where(is_local, tile_cols % row_blocks, tile_cols)
    key = tile_cols + jnp.where(is_local, n * row_blocks, 0)
    earlier = (key[None, :] < key[:, None]) | (
        (key[None, :] == key[:, None]) & (index[None, :] < index[:, None])
    )
    rank = jnp.sum(earlier.astype(jnp.int32), axis=1)
    placed = rank[None, :] == index[:, None]
    order = jnp.sum(jnp.where(placed, index[None, :], 0), axis=1)
    in_order = jnp.sum(jnp.where(placed, key[None, :], 0), axis=1)
    keep = jnp.concatenate([jnp.zeros((1,), F32), (in_order[1:] == in_order[:-1]).astype(F32)])
    dest = jnp.arange((n + 1) * row_blocks, dtype=jnp.int32)
    dest = jnp.where(dest < n * row_blocks, dest, dest + lax.axis_index("rows") * row_blocks)
    upto = jnp.sum((key[None, :] <= dest[:, None]).astype(jnp.int32), axis=1)
    below = jnp.sum((key[None, :] < dest[:, None]).astype(jnp.int32), axis=1)
    has = (upto > below).astype(F32)
    last = jnp.maximum(upto - 1, 0)

    smem = pl.BlockSpec(memory_space=pltpu.SMEM)
    vmem = pl.BlockSpec(memory_space=pltpu.VMEM)
    anywhere = pl.BlockSpec(memory_space=pl.ANY)
    dma = pltpu.SemaphoreType.DMA
    piece = width // n if sum_inside else 8
    hidden, grad_in, grad_w, grad_b = pl.pallas_call(
        functools.partial(kernel, n, chunks, sum_inside, scale),
        out_shape=(
            jax.ShapeDtypeStruct((width, nodes), BF16),
            jax.ShapeDtypeStruct((width, nodes), F32),
            jax.ShapeDtypeStruct((width, hid), F32),
            jax.ShapeDtypeStruct((1, width), F32),
        ),
        in_specs=[smem] * 5 + [vmem] + [anywhere] * 4,
        out_specs=(anywhere, anywhere, anywhere, vmem),
        scratch_shapes=[
            pltpu.VMEM((row_blocks, width, block), BF16),
            pltpu.VMEM((n * row_blocks, width, block), BF16),
            pltpu.VMEM((count, block, block), BF16),
            pltpu.VMEM((width, nodes), BF16),
            pltpu.VMEM((chunks, 4 * width, nodes // chunks), BF16),
            pltpu.VMEM((chunks, 4 * width, nodes // chunks), BF16),
            pltpu.VMEM((row_blocks, width, block), BF16),
            pltpu.VMEM((count, width, block), F32),
            pltpu.VMEM((count, width, block), F32),
            pltpu.VMEM((row_blocks, width, block), F32),
            pltpu.VMEM((width, nodes), BF16),
            pltpu.VMEM((width, nodes), F32),
            pltpu.VMEM((2, half, row_blocks, width, block), BF16),
            pltpu.VMEM((4 * width, hid), BF16),
            pltpu.VMEM((hid, 4 * width), BF16),
            pltpu.VMEM((width, block), F32),
            pltpu.VMEM((width, hid + block), F32),
            pltpu.VMEM((n if sum_inside else 1, piece, hid + block), F32),
            pltpu.VMEM((width, hid + block), F32),
            dma((3,)),
            dma((row_blocks,)),
            dma((2 + chunks,)),
            dma((3,)),
            dma((3,)),
            dma((2, half, chunks)),
            dma((2, half, chunks)),
            dma((2, 3, chunks)),
            dma((2, 3, chunks)),
            dma((2, half, chunks)),
            dma((2, half, chunks)),
            dma((n,)),
            dma((n,)),
            dma((n,)),
            dma((n,)),
        ],
        compiler_params=pltpu.CompilerParams(
            collective_id=0, has_side_effects=True, vmem_limit_bytes=52 * 1024 * 1024
        ),
        cost_estimate=pl.CostEstimate(
            flops=2 * 2 * count * width * block * block + 6 * width * hid * nodes,
            bytes_accessed=2 * count * block * block,
            transcendentals=width * nodes,
        ),
    )(
        cols,
        order,
            keep,
        last,
        has,
        bias[None, :],
        feats,
        weight,
        tile_values,
        cotangent,
    )
    bias_total = grad_b[0]
    if not sum_inside:
        grad_w, bias_total = lax.psum((grad_w * scale, bias_total * scale), "rows")
    return hidden, grad_in, grad_w, bias_total


def solution(mesh):
    placed = (
        P("feat", "rows"),
        P("feat", None),
        P("feat"),
        P("rows"),
        P("rows", None, None),
        P("feat", "rows"),
    )
    return jax.shard_map(
        local,
        mesh=mesh,
        in_specs=placed,
        out_specs=(P("feat", "rows"), P("feat", "rows"), P("feat", None), P("feat")),
        check_vma=False,
    )
```
